32 devices in a mesh: gx: 2 (over y), gy: 4 (over x, core), gz: 4 (over z).
Axes of the slice: x: 2, y: 2, z: 4, core: 2. Of those that a mesh axis runs over, the one named last changes fastest.
Arguments:
- pressure: float32 [32, 64, 512], P('gx', 'gy', 'gz'), may hold values from -6 to 6
- velocity: float32 [3, 32, 64, 512], P(None, 'gx', 'gy', 'gz'), may hold values from -6 to 6
- inv_density: float32 [32, 64, 512], P('gx', 'gy', 'gz'), may hold values from 0.5 to 2
- bulk: float32 [32, 64, 512], P('gx', 'gy', 'gz'), may hold values from 0.25 to 1
- node_weight: float32 [2, 4, 256], P('gx', 'gy'), may hold values from 0.2 to 2
- node_patch: int32 [2, 4, 256], P('gx', 'gy'), may hold values from 0 to 1023, as said below
- patch_slot: int32 [1024], replicated, may hold values from 0 to 1023, as said below
- gauge_x: int32 [256], replicated, may hold values from 0 to 31
- gauge_y: int32 [256], replicated, may hold values from 0 to 63
- gauge_misfit: float32 [4, 256], replicated, may hold values from -6 to 6
Outputs:
- pressure_out: float32 [32, 64, 512], P('gx', 'gy', 'gz')
- velocity_out: float32 [3, 32, 64, 512], P(None, 'gx', 'gy', 'gz')
- slip_grad: float32 [1024], P(('gx', 'gy', 'gz'))
The draws below stay inside these ranges and needn't reach their ends.
Inputs may be any that keep to these rules, and one draw needn't show every extreme that they name: `node_patch`: of the seafloor nodes of one tile, at most 128 map to patches whose slot lies in one owner's range of 128 slots; in every draw one owner receives exactly 128 from every tile. `patch_slot`: A permutation of the patches.
All inputs are finite; a program needn't handle non-finite values.
Results may differ from the reference program's by a relative error of at most 0.00018.
Values sent between devices are 32-bit elements; how exact they have to be, the bound alone decides.
A program may use at most 64 MiB of HBM per device.

```python
import math
import jax
import jax.numpy as jnp
from jax import lax

CX = 16
CY = 16
ITERS = 4
P_DEV = 128
GAUGES = 256
NX = 32
NY = 64
NZ = 512
SEA_DEV = 256
PATCHES = 1024
N_GX = 2
N_GY = 4


def route_tables(key):
    owners_count = N_GX * N_GY
    capacity = 4 * SEA_DEV // owners_count
    light_copies = max(capacity // 4, 1)
    popular_count = max(owners_count // 8, 1)
    ranking = jax.random.permutation(jax.random.fold_in(key, 11), owners_count).astype(jnp.int32)
    full_owner = ranking[0]
    popular = jnp.zeros((owners_count,), jnp.int32).at[ranking[1:1 + popular_count]].set(1)
    copies = jnp.where(popular == 1, capacity, light_copies).astype(jnp.int32)
    copies = copies.at[full_owner].set(0)
    element = jnp.arange(owners_count * capacity, dtype=jnp.int32)
    element_owner = element // capacity
    usable = element % capacity < copies[element_owner]
    remaining = SEA_DEV - capacity

    def one_device(device_key):
        key_score, key_place, key_patch = jax.random.split(device_key, 3)
        priority = jax.random.randint(key_score, (owners_count * capacity,), 0, 65536, dtype=jnp.int32) * (owners_count * capacity) + element
        priority = jnp.where(usable, priority, 2147483647)
        picked = lax.top_k(-priority, remaining)[1]
        chosen = jnp.concatenate([jnp.full((capacity,), full_owner, jnp.int32), element_owner[picked].astype(jnp.int32)])
        chosen = jax.random.permutation(key_place, chosen)
        within = jax.random.randint(key_patch, (SEA_DEV,), 0, P_DEV, dtype=jnp.int32)
        return (chosen * P_DEV + within).astype(jnp.int32)
    device_keys = jax.random.split(jax.random.fold_in(key, 12), owners_count)
    slots = jax.vmap(one_device)(device_keys).reshape(N_GX, N_GY, SEA_DEV)
    slot_of_patch = jax.random.permutation(jax.random.fold_in(key, 13), PATCHES).astype(jnp.int32)
    patch_at_slot = jnp.argsort(slot_of_patch).astype(jnp.int32)
    return (patch_at_slot[slots].astype(jnp.int32), slot_of_patch)


def draw_node_patch(key, part):
    return route_tables(key)[0]


def draw_patch_slot(key, part):
    return route_tables(key)[1]


def touch_ends(array, rng, least, high):
    longest = array.shape.index(max(array.shape))
    spots = []
    for shift in (0, 1):
        where = [jax.random.randint(jax.random.fold_in(rng, axis), (), 0, length) for axis, length in enumerate(array.shape)]
        where[longest] = (where[longest] + shift) % array.shape[longest]
        spots.append(tuple(where))
    return array.at[spots[0]].set(least).at[spots[1]].set(high)


def steps_of(own_key, dims, cuts, low, top_value):
    factor_of, own = 1.0, jax.random.fold_in(own_key, 6)
    for axis_at, blocks in cuts:
        heights = jnp.exp(jax.random.uniform(jax.random.fold_in(own, axis_at), (blocks,), jnp.float32, low / len(cuts), top_value / len(cuts)))
        factor_of = factor_of * jnp.repeat(heights, dims[axis_at] // blocks).reshape([-1 if axis == axis_at else 1 for axis in range(len(dims))])
    return factor_of


def bell_draw(key, extent, scale, limit, cuts=(), held_as=jnp.bfloat16):
    array = scale * jax.random.normal(key, extent, jnp.float32)
    if cuts:
        array = array * steps_of(key, extent, cuts, -0.22, 0.18)
    return jnp.clip(array, -limit, limit).astype(held_as)


def setup_inputs(seed: int = 0) -> dict:
    splits = jax.random.split(jax.random.key(seed), 11)
    pressure = bell_draw(splits[0], (NX, NY, NZ), 1.0, 6.0, ((0, 2), (1, 4), (2, 4)), jnp.float32)
    velocity = bell_draw(splits[1], (3, NX, NY, NZ), 1.0, 6.0, ((1, 2), (2, 4), (3, 4)), jnp.float32)
    inv_density = jnp.clip(jnp.exp(math.log(2.0) - 1.3862944 * jax.random.uniform(splits[2], (NX, NY, NZ), jnp.float32) ** steps_of(splits[2], (NX, NY, NZ), ((0, 2), (1, 4), (2, 4)), -0.2, 0.2)), 0.5, 2.0)
    bulk = jnp.clip(jnp.exp(math.log(1.0) - 1.3862944 * jax.random.uniform(splits[3], (NX, NY, NZ), jnp.float32) ** steps_of(splits[3], (NX, NY, NZ), ((0, 2), (1, 4), (2, 4)), -0.2, 0.2)), 0.25, 1.0)
    node_weight = jnp.clip(jnp.exp(math.log(2.0) - 2.3025851 * jax.random.uniform(splits[4], (N_GX, N_GY, SEA_DEV), jnp.float32) ** steps_of(splits[4], (N_GX, N_GY, SEA_DEV), ((0, 2), (1, 4)), -0.2, 0.2)), 0.2, 2.0)
    node_patch = draw_node_patch(jax.random.fold_in(splits[10], 71), 0)
    patch_slot = draw_patch_slot(jax.random.fold_in(splits[10], 71), 0)
    gauge_x = touch_ends(jax.random.randint(splits[7], (GAUGES,), 0, NX), jax.random.fold_in(splits[7], 1), 0, NX - 1).astype(jnp.int32)
    gauge_y = touch_ends(jax.random.randint(splits[8], (GAUGES,), 0, NY), jax.random.fold_in(splits[8], 1), 0, NY - 1).astype(jnp.int32)
    gauge_misfit = bell_draw(splits[9], (ITERS, GAUGES), 1.0, 6.0, (), jnp.float32)
    return dict(pressure=pressure, velocity=velocity, inv_density=inv_density, bulk=bulk, node_weight=node_weight, node_patch=node_patch, patch_slot=patch_slot, gauge_x=gauge_x, gauge_y=gauge_y, gauge_misfit=gauge_misfit)


time_step = 0.5


def depth_weights(levels, first_crust):
    ocean_last = levels == first_crust - 1
    crust_first = levels == first_crust
    weight_above = jnp.where(ocean_last, 0.5, jnp.where(crust_first, 1.0, 0.5)).astype(jnp.float32)
    weight_here = jnp.where(ocean_last, 0.5, jnp.where(crust_first, -1.5, 0.0)).astype(jnp.float32)
    weight_below = jnp.where(ocean_last, -1.0, jnp.where(crust_first, 0.5, -0.5)).astype(jnp.float32)
    return weight_above, weight_here, weight_below


def reference(pressure, velocity, inv_density, bulk, node_weight, node_patch, patch_slot, gauge_x, gauge_y, gauge_misfit):
    first_crust = NZ // 2
    weight_above, weight_here, weight_below = depth_weights(jnp.arange(NZ), first_crust)
    sources = jnp.zeros((ITERS, NX, NY), jnp.float32).at[:, gauge_x, gauge_y].add(gauge_misfit)
    seafloor = jnp.zeros((NX, NY), jnp.float32)
    for instant in range(ITERS):
        seafloor = seafloor + 0.5 * (pressure[:, :, first_crust - 1] + pressure[:, :, first_crust])
        padded = jnp.pad(pressure, 1)
        slope_x = 0.5 * (padded[2:, 1:-1, 1:-1] - padded[:-2, 1:-1, 1:-1])
        slope_y = 0.5 * (padded[1:-1, 2:, 1:-1] - padded[1:-1, :-2, 1:-1])
        slope_z = weight_above * padded[1:-1, 1:-1, 2:] + weight_here * pressure + weight_below * padded[1:-1, 1:-1, :-2]
        velocity = jnp.stack([velocity[0] - time_step * inv_density * slope_x,
                              velocity[1] - time_step * inv_density * slope_y,
                              velocity[2] - time_step * inv_density * slope_z])
        along_x = jnp.pad(velocity[0], ((1, 1), (0, 0), (0, 0)))
        along_y = jnp.pad(velocity[1], ((0, 0), (1, 1), (0, 0)))
        along_z = jnp.pad(velocity[2], ((0, 0), (0, 0), (1, 1)))
        spread = 0.5 * (along_x[2:] - along_x[:-2]) + 0.5 * (along_y[:, 2:] - along_y[:, :-2]) + (
            weight_above * along_z[:, :, 2:] + weight_here * velocity[2] + weight_below * along_z[:, :, :-2])
        pressure = pressure - time_step * bulk * spread
        pressure = pressure.at[:, :, 0].add(time_step * sources[instant])
    tiles = jnp.transpose(seafloor.reshape(N_GX, CX, N_GY, CY), (0, 2, 1, 3)).reshape(N_GX, N_GY, SEA_DEV)
    node_values = node_weight * tiles
    slots = patch_slot[node_patch]
    slip_grad = jax.ops.segment_sum(node_values.reshape(-1), slots.reshape(-1), num_segments=PATCHES)
    return pressure, velocity, slip_grad
```

```python
import functools

import jax
import jax.numpy as jnp
from jax import lax
from jax.experimental import pallas as pl
from jax.experimental.pallas import tpu as pltpu
from jax.sharding import PartitionSpec as P

ITERS = 4
MESH_ID = pl.DeviceIdType.MESH
AXES = ("gx", "gy", "gz")
YA = 8
F32 = jnp.float32
HIGHEST = lax.Precision.HIGHEST
NT = (((1,), (1,)), ((), ()))


def kernel(
    sizes,
    p_in,
    v_in,
    d_in,
    b_in,
    weight_ref,
    patch_ref,
    slot_ref,
    gx_ref,
    gy_ref,
    misfit_ref,
    p_out,
    v_out,
    slip_out,
    p_ext,
    vx,
    vy,
    vz,
    inv,
    inv_y,
    bulk,
    pack_edge,
    vz_edge,
    fill_p,
    fill_v,
    y_send,
    y_recv,
    z_send,
    z_recv,
    yi_send,
    yi_recv,
    zi_send,
    zi_recv,
    source,
    slot_hot,
    spread_hot,
    part,
    got,
    load_sem,
    store_sem,
    send_sem,
    recv_sem,
    init_send,
    init_recv,
    slip_send,
    slip_recv,
):
    n_x, n_y, n_z = sizes
    rows_x, rows_y, depth = p_in.shape
    cells = rows_x * rows_y
    halves = rows_y // 8
    me = [lax.axis_index(a) for a in AXES]
    tiles = n_x * n_y
    tile = me[0] * n_y + me[1]
    root = n_z // 2
    has = {}
    other = {}
    for a in range(3):
        has[a, 0] = me[a] > 0
        has[a, 1] = me[a] < sizes[a] - 1
        for side in (0, 1):
            to = list(me)
            to[a] = me[a] + (2 * side - 1)
            other[a, side] = tuple(to)
    faces = [(a, side) for a in range(3) for side in (0, 1) if sizes[a] > 1]

    y_in = pl.ds(YA, rows_y)
    x_in = pl.ds(2, rows_x)
    loads = [
        pltpu.make_async_copy(p_in, p_ext.at[0, x_in, y_in], load_sem.at[0]),
        pltpu.make_async_copy(d_in, inv.at[pl.ds(1, rows_x)], load_sem.at[1]),
        pltpu.make_async_copy(v_in.at[2], vz, load_sem.at[2]),
        pltpu.make_async_copy(v_in.at[1], vy.at[:, y_in], load_sem.at[3]),
        pltpu.make_async_copy(v_in.at[0], vx.at[pl.ds(1, rows_x)], load_sem.at[4]),
        pltpu.make_async_copy(b_in, bulk, load_sem.at[5]),
    ]
    for load in loads:
        load.start()

    barrier = pltpu.get_barrier_semaphore()
    for f in faces:

        @pl.when(has[f])
        def _(f=f):
            pl.semaphore_signal(barrier, inc=1, device_id=other[f], device_id_type=MESH_ID)

    is_sender = (me[2] == root) | (me[2] == root - 1)
    my_sender = jnp.where(me[2] >= root, root, root - 1)

    def greet(t, _):
        @pl.when((t != tile) | (me[2] != my_sender))
        def _():
            pl.semaphore_signal(
                barrier, inc=1, device_id=(t // n_y, t % n_y, my_sender), device_id_type=MESH_ID
            )

        return 0

    lax.fori_loop(0, tiles, greet, 0)

    for side in (0, 1):

        @pl.when(jnp.logical_not(has[0, side]))
        def _(side=side):
            at = 0 if side == 0 else rows_x + 2
            p_ext[:, pl.ds(at, 2), :, :] = jnp.zeros_like(p_ext[:, pl.ds(at, 2), :, :])
            one = 0 if side == 0 else rows_x + 1
            vx[one] = jnp.zeros_like(vx[one])
            inv[one] = jnp.zeros_like(inv[one])

        @pl.when(jnp.logical_not(has[1, side]))
        def _(side=side):
            y_recv[:, side] = jnp.zeros_like(y_recv[:, side])
            yi_recv[side] = jnp.zeros_like(yi_recv[side])

        @pl.when(jnp.logical_not(has[2, side]))
        def _(side=side):
            z_recv[:, side] = jnp.zeros_like(z_recv[:, side])
            zi_recv[side] = jnp.zeros_like(zi_recv[side])

    lane = lax.broadcasted_iota(jnp.int32, (8, depth), 1)
    quad = lane & 3
    group = lane >> 2

    def packed(read):
        q = jnp.zeros((8, depth), F32)
        for j in range(rows_x * halves):
            rolled = pltpu.roll(read(j // halves, (j % halves) * 8), (4 * j + 2) % depth, 1)
            q = jnp.where(group == j, rolled, q)
        return q

    def unpack(tile_value, ref):
        for j in range(rows_x * halves):
            ref[j // halves, pl.ds((j % halves) * 8, 8), :] = pltpu.roll(
                tile_value, (-(4 * j + 2)) % depth, 1
            )

    def coefs(level):
        first = root * depth
        last_ocean = level == first - 1
        crust = level == first
        up = jnp.where(crust, 1.0, 0.5).astype(F32)
        mid = jnp.where(last_ocean, 0.5, jnp.where(crust, -1.5, 0.0)).astype(F32)
        low = jnp.where(last_ocean, -1.0, jnp.where(crust, 0.5, -0.5)).astype(F32)
        return up, mid, low

    row_lane = lax.broadcasted_iota(jnp.int32, (1, 1, depth), 2)
    up, mid, low = coefs(me[2] * depth + row_lane)
    up_e, mid_e, low_e = coefs(
        jnp.where(quad == 1, me[2] * depth - 1, (me[2] + 1) * depth)
    )

    def copy_x(s, side, to):
        src, dst = (2, rows_x + 2) if side == 0 else (rows_x, 0)
        return pltpu.make_async_remote_copy(
            src_ref=p_ext.at[s, pl.ds(src, 2), y_in],
            dst_ref=p_ext.at[s, pl.ds(dst, 2), y_in],
            send_sem=send_sem.at[s, side],
            recv_sem=recv_sem.at[s, 1 - side],
            device_id=to,
            device_id_type=MESH_ID,
        )

    def copy_y(s, side, to):
        return pltpu.make_async_remote_copy(
            src_ref=y_send.at[s, side],
            dst_ref=y_recv.at[s, 1 - side],
            send_sem=send_sem.at[s, 2 + side],
            recv_sem=recv_sem.at[s, 3 - side],
            device_id=to,
            device_id_type=MESH_ID,
        )

    def copy_z(s, side, to):
        return pltpu.make_async_remote_copy(
            src_ref=z_send.at[s],
            dst_ref=z_recv.at[s, 1 - side],
            send_sem=send_sem.at[s, 4 + side],
            recv_sem=recv_sem.at[s, 5 - side],
            device_id=to,
            device_id_type=MESH_ID,
        )

    step_copies = {0: copy_x, 1: copy_y, 2: copy_z}

    def init_copy(src, dst, to, n, back):
        return pltpu.make_async_remote_copy(
            src_ref=src,
            dst_ref=dst,
            send_sem=init_send.at[n],
            recv_sem=init_recv.at[back],
            device_id=to,
            device_id_type=MESH_ID,
        )

    def init_copies(a, side, to):
        if a == 0:
            src, dst = (0, rows_x + 1) if side == 0 else (rows_x - 1, 0)
            return [
                init_copy(
                    v_in.at[0, pl.ds(src, 1)], vx.at[pl.ds(dst, 1)], to, side, 1 - side
                ),
                init_copy(
                    inv.at[pl.ds(src + 1, 1)], inv.at[pl.ds(dst, 1)], to, 6 + side, 7 - side
                ),
            ]
        if a == 1:
            return [init_copy(yi_send.at[side], yi_recv.at[1 - side], to, 2 + side, 3 - side)]
        return [init_copy(zi_send, zi_recv.at[1 - side], to, 4 + side, 5 - side)]

    def send(s):
        z_send[s] = packed(lambda x, y: p_ext[s, 2 + x, pl.ds(YA + y, 8), :])
        y_send[s, 0] = p_ext[s, 2 : rows_x + 2, YA : YA + 2, :]
        y_send[s, 1] = p_ext[s, 2 : rows_x + 2, YA + rows_y - 2 : YA + rows_y, :]
        for f in faces:

            @pl.when(has[f])
            def _(f=f):
                step_copies[f[0]](s, f[1], other[f]).start()

    def receive(s):
        for f in faces:

            @pl.when(has[f])
            def _(f=f):
                step_copies[f[0]](s, 1 - f[1], other[f]).wait_recv()

        p_ext[s, 2 : rows_x + 2, YA - 2 : YA, :] = y_recv[s, 0]
        p_ext[s, 2 : rows_x + 2, YA + rows_y : YA + rows_y + 2, :] = y_recv[s, 1]

    def update(s, sea, end):
        own = z_send[s]
        halo = jnp.where(quad < 2, z_recv[s, 0], z_recv[s, 1])
        sea = sea + jnp.where(
            me[2] >= root,
            jnp.where(quad == 2, own, halo),
            jnp.where(quad == 2, halo, own),
        )
        above = pltpu.roll(jnp.where(quad == 2, own, halo), depth - 1, 1)
        below = pltpu.roll(jnp.where(quad == 1, own, halo), 1, 1)
        edge = vz_edge[...] - 0.5 * pack_edge[...] * (
            up_e * above + mid_e * halo + low_e * below
        )
        vz_edge[...] = edge
        unpack(halo, fill_p)
        unpack(edge, fill_v)

        if end is not None:
            end(sea)

        def along_x(i, _):
            at = pl.ds(i * 3, 3)
            ahead = p_ext[s, pl.ds(i * 3 + 2, 3), y_in, :]
            behind = p_ext[s, pl.ds(i * 3, 3), y_in, :]
            vx[at] = vx[at] - 0.25 * inv[at] * (ahead - behind)
            return 0

        for i in range((rows_x + 2) // 3):
            along_x(i, 0)
        inner = slice(2, rows_x + 2)
        vy[:, YA - 1 : YA, :] = vy[:, YA - 1 : YA, :] - 0.25 * inv_y[0] * (
            p_ext[s, inner, YA : YA + 1, :] - p_ext[s, inner, YA - 2 : YA - 1, :]
        )
        end_y = YA + rows_y
        vy[:, end_y : end_y + 1, :] = vy[:, end_y : end_y + 1, :] - 0.25 * inv_y[1] * (
            p_ext[s, inner, end_y + 1 : end_y + 2, :] - p_ext[s, inner, end_y - 1 : end_y, :]
        )
        chunk = 4
        for i in range(0, rows_x, chunk):
            at = pl.ds(i, chunk)
            at_p = pl.ds(i + 2, chunk)
            here = p_ext[s, at_p, y_in, :]
            rho = inv[pl.ds(i + 1, chunk)]
            vy[at, y_in, :] = vy[at, y_in, :] - 0.25 * rho * (
                p_ext[s, at_p, pl.ds(YA + 1, rows_y), :] - p_ext[s, at_p, pl.ds(YA - 1, rows_y), :]
            )
            halo_p = fill_p[at]
            above_p = pltpu.roll(jnp.where(row_lane == 0, halo_p, here), depth - 1, 2)
            below_p = pltpu.roll(jnp.where(row_lane == depth - 1, halo_p, here), 1, 2)
            vz[at] = vz[at] - 0.5 * rho * (up * above_p + mid * here + low * below_p)
        for i in range(0, rows_x, chunk):
            at = pl.ds(i, chunk)
            at_p = pl.ds(i + 2, chunk)
            w = vz[at]
            halo_v = fill_v[at]
            above_v = pltpu.roll(jnp.where(row_lane == 0, halo_v, w), depth - 1, 2)
            below_v = pltpu.roll(jnp.where(row_lane == depth - 1, halo_v, w), 1, 2)
            spread = (
                0.5 * (vx[pl.ds(i + 2, chunk)] - vx[at])
                + 0.5 * (vy[at, pl.ds(YA + 1, rows_y), :] - vy[at, pl.ds(YA - 1, rows_y), :])
                + (up * above_v + mid * w + low * below_v)
            )
            added = jnp.where(row_lane == 0, pltpu.roll(source[at], (depth - s) % depth, 2), 0.0)
            p_ext[s + 1, at_p, y_in, :] = p_ext[s, at_p, y_in, :] - 0.5 * bulk[at] * spread + added
        return sea

    for load in loads:
        load.wait()
    zi_send[0] = packed(lambda x, y: vz[x, pl.ds(y, 8), :])
    zi_send[1] = packed(lambda x, y: inv[1 + x, pl.ds(y, 8), :])
    for side, y in ((0, 0), (1, rows_y - 1)):
        yi_send[side, :, 0:1, :] = vy[:, YA + y : YA + y + 1, :]
        yi_send[side, :, 1:2, :] = inv[1 : rows_x + 1, y : y + 1, :]
    count = sum(has[f].astype(jnp.int32) for f in faces)
    owners_z = jnp.where(me[2] == root, n_z - root, jnp.where(me[2] == root - 1, root, 0))
    count = count + jnp.where(is_sender, owners_z * tiles - 1, 0)
    pl.semaphore_wait(barrier, count)
    send(0)
    for f in faces:

        @pl.when(has[f])
        def _(f=f):
            for copy in init_copies(*f, other[f]):
                copy.start()

    cell_x = gx_ref[...] - me[0] * rows_x
    cell_y = gy_ref[...] - me[1] * rows_y
    inside = (cell_x >= 0) & (cell_x < rows_x) & (cell_y >= 0) & (cell_y < rows_y)
    cell = jnp.where(inside, cell_x * rows_y + cell_y, -1)
    gauges = cell.shape[1]
    hot = (lax.broadcasted_iota(jnp.int32, (cells, gauges), 0) == cell).astype(F32)
    scaled = misfit_ref[...] * jnp.where(me[2] == 0, 0.5, 0.0).astype(F32)
    scaled = jnp.concatenate([scaled, jnp.zeros((depth - ITERS, gauges), F32)], axis=0)
    planes = lax.dot_general(hot, scaled, NT, precision=HIGHEST, preferred_element_type=F32)
    source[...] = planes.reshape(rows_x, rows_y, depth)

    nodes = patch_ref.shape[-1]
    patches = slot_ref.shape[1]
    per = patches // tiles
    shift = per.bit_length() - 1
    assert per == 1 << shift and per == 128
    block = min(patches, 1024)
    patch = patch_ref[...].reshape(1, nodes)
    slot_parts = jnp.zeros((8, nodes), F32)
    first_row = lax.broadcasted_iota(jnp.int32, (8, block), 0) == 0
    for at in range(0, patches, block):
        slots = slot_ref[:, at : at + block]
        table = jnp.where(first_row, slots >> shift, slots & (per - 1)).astype(F32)
        hot = lax.broadcasted_iota(jnp.int32, (block, nodes), 0) + at == patch
        slot_parts = slot_parts + jnp.dot(
            table.astype(jnp.bfloat16),
            hot.astype(F32).astype(jnp.bfloat16),
            preferred_element_type=F32,
        )
    slot = (slot_parts[0:1] * per + slot_parts[1:2]).astype(jnp.int32)
    for at in range(0, patches, block):
        hot = lax.broadcasted_iota(jnp.int32, (block, nodes), 0) + at == slot
        slot_hot[pl.ds(at, block), :] = hot.astype(F32).astype(jnp.bfloat16)
    node = lax.broadcasted_iota(jnp.int32, (depth, nodes), 1)
    spread_hot[...] = (
        lax.broadcasted_iota(jnp.int32, (depth, nodes), 0) == 4 * (node >> 3) + 2
    ).astype(F32)

    def slip_copy(o, c):
        return pltpu.make_async_remote_copy(
            src_ref=part.at[o],
            dst_ref=got.at[tile],
            send_sem=slip_send.at[o, c],
            recv_sem=slip_recv.at[tile],
            device_id=(o // n_y, o % n_y, c),
            device_id_type=MESH_ID,
        )

    def to_owners(act):
        def one(n, _):
            o = n // n_z
            c = n % n_z
            mine = (c >= root) == (me[2] >= root)

            @pl.when(mine & ((o != tile) | (c != me[2])))
            def _():
                act(slip_copy(o, c))

            return 0

        lax.fori_loop(0, tiles * n_z, one, 0)

    def finish_sea(sea):
        @pl.when(is_sender)
        def _():
            total = 0.5 * (sea + pltpu.roll(sea, 1, 1))
            values = jnp.dot(total, spread_hot[...], precision=HIGHEST, preferred_element_type=F32)
            sub = lax.broadcasted_iota(jnp.int32, (8, nodes), 0)
            col = lax.broadcasted_iota(jnp.int32, (8, nodes), 1)
            row = jnp.sum(jnp.where((col & 7) == sub, values, 0.0), axis=0, keepdims=True)
            row = row * weight_ref[...].reshape(1, nodes)
            high = row.astype(jnp.bfloat16).astype(F32)
            rest = row - high
            middle = rest.astype(jnp.bfloat16).astype(F32)
            lowest = rest - middle
            split = jnp.where(
                sub == 0, high, jnp.where(sub == 1, middle, jnp.where(sub == 2, lowest, 0.0))
            ).astype(jnp.bfloat16)
            for at in range(0, patches, block):
                sums = lax.dot_general(
                    split, slot_hot[pl.ds(at, block), :], NT, preferred_element_type=F32
                )
                sums = jnp.sum(sums, axis=0, keepdims=True)
                for o in range(block // per):
                    part[at // per + o] = sums[:, o * per : (o + 1) * per]
            got[tile] = part[tile]
            to_owners(lambda copy: copy.start())

    for f in faces:

        @pl.when(has[f])
        def _(f=f):
            for copy in init_copies(f[0], 1 - f[1], other[f]):
                copy.wait_recv()

    for side, y in ((0, YA - 1), (1, YA + rows_y)):
        vy[:, y : y + 1, :] = yi_recv[side, :, 0:1, :]
        inv_y[side] = yi_recv[side, :, 1:2, :]
    kept = (quad == 1) | (quad == 2)
    vz_edge[...] = jnp.where(
        kept, jnp.where(quad == 1, zi_recv[0, 0], zi_recv[1, 0]), 0.0
    )
    pack_edge[...] = jnp.where(
        kept, jnp.where(quad == 1, zi_recv[0, 1], zi_recv[1, 1]), 0.0
    )

    receive(0)
    sea = update(0, jnp.zeros((8, depth), F32), None)
    for s in range(1, ITERS):
        send(s)
        receive(s)
        sea = update(s, sea, finish_sea if s == ITERS - 1 else None)

    stores = [
        pltpu.make_async_copy(vx.at[pl.ds(1, rows_x)], v_out.at[0], store_sem.at[0]),
        pltpu.make_async_copy(vy.at[:, y_in], v_out.at[1], store_sem.at[1]),
        pltpu.make_async_copy(vz, v_out.at[2], store_sem.at[2]),
        pltpu.make_async_copy(p_ext.at[ITERS, x_in, y_in], p_out, store_sem.at[3]),
    ]
    for store in stores:
        store.start()

    def arrive(t, _):
        @pl.when((t != tile) | (me[2] != my_sender))
        def _():
            pltpu.make_async_remote_copy(
                src_ref=part.at[0],
                dst_ref=got.at[t],
                send_sem=slip_send.at[0, 0],
                recv_sem=slip_recv.at[t],
                device_id=(t // n_y, t % n_y, my_sender),
                device_id_type=MESH_ID,
            ).wait_recv()

        return 0

    lax.fori_loop(0, tiles, arrive, 0)
    total = jnp.sum(got[...], axis=0)
    piece = per // n_z
    picked = total[:, 0:piece]
    for c in range(1, n_z):
        picked = jnp.where(me[2] == c, total[:, c * piece : (c + 1) * piece], picked)
    slip_out[...] = picked

    for f in faces:

        @pl.when(has[f])
        def _(f=f):
            for copy in init_copies(*f, other[f]):
                copy.wait_send()
            for s in range(ITERS):
                step_copies[f[0]](s, f[1], other[f]).wait_send()

    @pl.when(is_sender)
    def _():
        to_owners(lambda copy: copy.wait_send())

    for store in stores:
        store.wait()


def local(sizes, pressure, velocity, inv_density, bulk, node_weight, node_patch, patch_slot,
          gauge_x, gauge_y, gauge_misfit):
    rows_x, rows_y, depth = pressure.shape
    n_x, n_y, n_z = sizes
    tiles = n_x * n_y
    nodes = node_patch.shape[-1]
    patches = patch_slot.shape[0]
    per = patches // tiles
    wide_y = rows_y + 2 * YA
    box = (rows_x, rows_y, depth)
    vmem = pl.BlockSpec(memory_space=pltpu.VMEM)
    hbm = pl.BlockSpec(memory_space=pl.ANY)
    scratch = [
        pltpu.VMEM((ITERS + 1, rows_x + 4, wide_y, depth), F32),
        pltpu.VMEM((rows_x + 2, rows_y, depth), F32),
        pltpu.VMEM((rows_x, wide_y, depth), F32),
        pltpu.VMEM(box, F32),
        pltpu.VMEM((rows_x + 2, rows_y, depth), F32),
        pltpu.VMEM((2, rows_x, 1, depth), F32),
        pltpu.VMEM(box, F32),
        pltpu.VMEM((8, depth), F32),
        pltpu.VMEM((8, depth), F32),
        pltpu.VMEM(box, F32),
        pltpu.VMEM(box, F32),
        pltpu.VMEM((ITERS, 2, rows_x, 2, depth), F32),
        pltpu.VMEM((ITERS, 2, rows_x, 2, depth), F32),
        pltpu.VMEM((ITERS, 8, depth), F32),
        pltpu.VMEM((ITERS, 2, 8, depth), F32),
        pltpu.VMEM((2, rows_x, 2, depth), F32),
        pltpu.VMEM((2, rows_x, 2, depth), F32),
        pltpu.VMEM((2, 8, depth), F32),
        pltpu.VMEM((2, 2, 8, depth), F32),
        pltpu.VMEM(box, F32),
        pltpu.VMEM((patches, nodes), jnp.bfloat16),
        pltpu.VMEM((depth, nodes), F32),
        pltpu.VMEM((tiles, 1, per), F32),
        pltpu.VMEM((tiles, 1, per), F32),
        pltpu.SemaphoreType.DMA((6,)),
        pltpu.SemaphoreType.DMA((4,)),
        pltpu.SemaphoreType.DMA((ITERS, 6)),
        pltpu.SemaphoreType.DMA((ITERS, 6)),
        pltpu.SemaphoreType.DMA((8,)),
        pltpu.SemaphoreType.DMA((8,)),
        pltpu.SemaphoreType.DMA((tiles, n_z)),
        pltpu.SemaphoreType.DMA((tiles,)),
    ]
    p_new, v_new, slip = pl.pallas_call(
        functools.partial(kernel, sizes),
        out_shape=[
            jax.ShapeDtypeStruct(box, F32),
            jax.ShapeDtypeStruct((3,) + box, F32),
            jax.ShapeDtypeStruct((1, per // n_z), F32),
        ],
        in_specs=[hbm] * 4 + [vmem] * 6,
        out_specs=[hbm, hbm, vmem],
        scratch_shapes=scratch,
        compiler_params=pltpu.CompilerParams(
            collective_id=0, has_side_effects=True, vmem_limit_bytes=32 * 1024 * 1024
        ),
    )(
        pressure,
        velocity,
        inv_density,
        bulk,
        node_weight,
        node_patch,
        patch_slot.reshape(1, patches),
        gauge_x.reshape(1, -1),
        gauge_y.reshape(1, -1),
        gauge_misfit,
    )
    return p_new, v_new, slip.reshape(per // n_z)


def solution(mesh):
    placed = (
        P("gx", "gy", "gz"),
        P(None, "gx", "gy", "gz"),
        P("gx", "gy", "gz"),
        P("gx", "gy", "gz"),
        P("gx", "gy", None),
        P("gx", "gy", None),
        P(),
        P(),
        P(),
        P(),
    )
    sizes = tuple(mesh.shape[a] for a in AXES)
    return jax.shard_map(
        functools.partial(local, sizes),
        mesh=mesh,
        in_specs=placed,
        out_specs=(P("gx", "gy", "gz"), P(None, "gx", "gy", "gz"), P(("gx", "gy", "gz"))),
        check_vma=False,
    )
```

```python
import functools

import jax
import jax.numpy as jnp
from jax import lax
from jax.experimental import pallas as pl
from jax.experimental.pallas import tpu as pltpu
from jax.sharding import PartitionSpec as P

ITERS = 4
MESH_ID = pl.DeviceIdType.MESH
AXES = ("gx", "gy", "gz")
YA = 8
F32 = jnp.float32
HIGHEST = lax.Precision.HIGHEST
NT = (((1,), (1,)), ((), ()))


def kernel(
    sizes,
    p_in,
    v_in,
    d_in,
    b_in,
    weight_in,
    patch_in,
    slot_in,
    gx_in,
    gy_in,
    misfit_in,
    p_out,
    v_out,
    slip_out,
    weight_ref,
    patch_ref,
    slot_ref,
    gx_ref,
    gy_ref,
    misfit_ref,
    p_ext,
    vx,
    vy,
    vz,
    inv,
    inv_y,
    bulk,
    pack_edge,
    vz_edge,
    fill_p,
    fill_v,
    y_send,
    y_recv,
    z_send,
    z_recv,
    yi_send,
    yi_recv,
    zi_send,
    zi_recv,
    source,
    slot_hot,
    spread_hot,
    part,
    got,
    total,
    got_all,
    load_sem,
    send_sem,
    recv_sem,
    init_send,
    init_recv,
    slip_send,
    slip_recv,
    depth_send,
    depth_recv,
):
    n_x, n_y, n_z = sizes
    rows_x, rows_y, depth = p_in.shape
    cells = rows_x * rows_y
    halves = rows_y // 8
    me = [lax.axis_index(a) for a in AXES]
    tiles = n_x * n_y
    tile = me[0] * n_y + me[1]
    root = n_z // 2
    has = {}
    other = {}
    for a in range(3):
        has[a, 0] = me[a] > 0
        has[a, 1] = me[a] < sizes[a] - 1
        for side in (0, 1):
            to = list(me)
            to[a] = me[a] + (2 * side - 1)
            other[a, side] = tuple(to)
    faces = [(a, side) for a in range(3) for side in (0, 1) if sizes[a] > 1]

    y_in = pl.ds(YA, rows_y)
    x_in = pl.ds(2, rows_x)
    loads = [
        pltpu.make_async_copy(p_in, p_ext.at[0, x_in, y_in], load_sem.at[0]),
        pltpu.make_async_copy(d_in, inv.at[pl.ds(1, rows_x)], load_sem.at[1]),
        pltpu.make_async_copy(v_in.at[2], vz, load_sem.at[2]),
        pltpu.make_async_copy(v_in.at[1], vy.at[:, y_in], load_sem.at[3]),
        pltpu.make_async_copy(v_in.at[0], vx.at[pl.ds(1, rows_x)], load_sem.at[4]),
        pltpu.make_async_copy(b_in, bulk, load_sem.at[5]),
        pltpu.make_async_copy(weight_in, weight_ref, load_sem.at[6]),
        pltpu.make_async_copy(patch_in, patch_ref, load_sem.at[7]),
        pltpu.make_async_copy(slot_in, slot_ref, load_sem.at[8]),
        pltpu.make_async_copy(gx_in, gx_ref, load_sem.at[9]),
        pltpu.make_async_copy(gy_in, gy_ref, load_sem.at[10]),
        pltpu.make_async_copy(misfit_in, misfit_ref, load_sem.at[11]),
    ]
    for load in loads:
        load.start()

    barrier = pltpu.get_barrier_semaphore()
    for f in faces:

        @pl.when(has[f])
        def _(f=f):
            pl.semaphore_signal(barrier, inc=1, device_id=other[f], device_id_type=MESH_ID)

    at_sea = (me[2] == root) | (me[2] == root - 1)

    def each_tile(act):
        def one(o_x, o_y):
            @pl.when((o_x != me[0]) | (o_y != me[1]))
            def _():
                act(o_x, o_y)

        if tiles <= 8:
            for o in range(tiles):
                one(o // n_y, o % n_y)
        else:

            def row(o_x, _):
                def column(o_y, _):
                    one(o_x, o_y)
                    return 0

                return lax.fori_loop(0, n_y, column, 0)

            lax.fori_loop(0, n_x, row, 0)

    def greet(o_x, o_y):
        pl.semaphore_signal(
            barrier, inc=1, device_id=(o_x, o_y, me[2]), device_id_type=MESH_ID
        )

    @pl.when(at_sea)
    def _():
        each_tile(greet)

    for c in (root - 1, root):

        @pl.when(me[2] != c)
        def _(c=c):
            pl.semaphore_signal(
                barrier, inc=1, device_id=(me[0], me[1], c), device_id_type=MESH_ID
            )

    for side in (0, 1):

        @pl.when(jnp.logical_not(has[0, side]))
        def _(side=side):
            at = 0 if side == 0 else rows_x + 2
            p_ext[:, pl.ds(at, 2), :, :] = jnp.zeros_like(p_ext[:, pl.ds(at, 2), :, :])
            one = 0 if side == 0 else rows_x + 1
            vx[one] = jnp.zeros_like(vx[one])
            inv[one] = jnp.zeros_like(inv[one])

        @pl.when(jnp.logical_not(has[1, side]))
        def _(side=side):
            y_recv[:, side] = jnp.zeros_like(y_recv[:, side])
            yi_recv[side] = jnp.zeros_like(yi_recv[side])

        @pl.when(jnp.logical_not(has[2, side]))
        def _(side=side):
            z_recv[:, side] = jnp.zeros_like(z_recv[:, side])
            zi_recv[side] = jnp.zeros_like(zi_recv[side])

    lane = lax.broadcasted_iota(jnp.int32, (8, depth), 1)
    quad = lane & 3
    group = lane >> 2

    def packed(read):
        q = jnp.zeros((8, depth), F32)
        for j in range(rows_x * halves):
            rolled = pltpu.roll(read(j // halves, (j % halves) * 8), (4 * j + 2) % depth, 1)
            q = jnp.where(group == j, rolled, q)
        return q

    def unpack(tile_value, ref):
        for j in range(rows_x * halves):
            ref[j // halves, pl.ds((j % halves) * 8, 8), :] = pltpu.roll(
                tile_value, (-(4 * j + 2)) % depth, 1
            )

    def coefs(level):
        first = root * depth
        last_ocean = level == first - 1
        crust = level == first
        up = jnp.where(crust, 1.0, 0.5).astype(F32)
        mid = jnp.where(last_ocean, 0.5, jnp.where(crust, -1.5, 0.0)).astype(F32)
        low = jnp.where(last_ocean, -1.0, jnp.where(crust, 0.5, -0.5)).astype(F32)
        return up, mid, low

    row_lane = lax.broadcasted_iota(jnp.int32, (1, 1, depth), 2)
    up, mid, low = coefs(me[2] * depth + row_lane)
    up_e, mid_e, low_e = coefs(
        jnp.where(quad == 1, me[2] * depth - 1, (me[2] + 1) * depth)
    )

    def copy_x(s, side, to):
        src, dst = (2, rows_x + 2) if side == 0 else (rows_x, 0)
        return pltpu.make_async_remote_copy(
            src_ref=p_ext.at[s, pl.ds(src, 2), y_in],
            dst_ref=p_ext.at[s, pl.ds(dst, 2), y_in],
            send_sem=send_sem.at[s, side],
            recv_sem=recv_sem.at[s, 1 - side],
            device_id=to,
            device_id_type=MESH_ID,
        )

    def copy_y(s, side, to):
        return pltpu.make_async_remote_copy(
            src_ref=y_send.at[s, side],
            dst_ref=y_recv.at[s, 1 - side],
            send_sem=send_sem.at[s, 2 + side],
            recv_sem=recv_sem.at[s, 3 - side],
            device_id=to,
            device_id_type=MESH_ID,
        )

    def copy_z(s, side, to):
        return pltpu.make_async_remote_copy(
            src_ref=z_send.at[s],
            dst_ref=z_recv.at[s, 1 - side],
            send_sem=send_sem.at[s, 4 + side],
            recv_sem=recv_sem.at[s, 5 - side],
            device_id=to,
            device_id_type=MESH_ID,
        )

    step_copies = {0: copy_x, 1: copy_y, 2: copy_z}

    def init_copy(src, dst, to, n, back):
        return pltpu.make_async_remote_copy(
            src_ref=src,
            dst_ref=dst,
            send_sem=init_send.at[n],
            recv_sem=init_recv.at[back],
            device_id=to,
            device_id_type=MESH_ID,
        )

    def init_copies(a, side, to):
        if a == 0:
            src, dst = (0, rows_x + 1) if side == 0 else (rows_x - 1, 0)
            return [
                init_copy(
                    v_in.at[0, pl.ds(src, 1)], vx.at[pl.ds(dst, 1)], to, side, 1 - side
                ),
                init_copy(
                    inv.at[pl.ds(src + 1, 1)], inv.at[pl.ds(dst, 1)], to, 6 + side, 7 - side
                ),
            ]
        if a == 1:
            return [init_copy(yi_send.at[side], yi_recv.at[1 - side], to, 2 + side, 3 - side)]
        return [init_copy(zi_send, zi_recv.at[1 - side], to, 4 + side, 5 - side)]

    def send(s):
        z_send[s] = packed(lambda x, y: p_ext[s, 2 + x, pl.ds(YA + y, 8), :])
        y_send[s, 0] = p_ext[s, 2 : rows_x + 2, YA : YA + 2, :]
        y_send[s, 1] = p_ext[s, 2 : rows_x + 2, YA + rows_y - 2 : YA + rows_y, :]
        for f in faces:

            @pl.when(has[f])
            def _(f=f):
                step_copies[f[0]](s, f[1], other[f]).start()

    def receive(s):
        for f in faces:

            @pl.when(has[f])
            def _(f=f):
                step_copies[f[0]](s, 1 - f[1], other[f]).wait_recv()

        p_ext[s, 2 : rows_x + 2, YA - 2 : YA, :] = y_recv[s, 0]
        p_ext[s, 2 : rows_x + 2, YA + rows_y : YA + rows_y + 2, :] = y_recv[s, 1]

    def update(s, last):
        own = z_send[s]
        halo = jnp.where(quad < 2, z_recv[s, 0], z_recv[s, 1])
        above = pltpu.roll(jnp.where(quad == 2, own, halo), depth - 1, 1)
        below = pltpu.roll(jnp.where(quad == 1, own, halo), 1, 1)
        edge = vz_edge[...] - 0.5 * pack_edge[...] * (
            up_e * above + mid_e * halo + low_e * below
        )
        vz_edge[...] = edge
        unpack(halo, fill_p)
        unpack(edge, fill_v)

        def along_x(i, _):
            at = pl.ds(i * 3, 3)
            ahead = p_ext[s, pl.ds(i * 3 + 2, 3), y_in, :]
            behind = p_ext[s, pl.ds(i * 3, 3), y_in, :]
            vx[at] = vx[at] - 0.25 * inv[at] * (ahead - behind)
            return 0

        for i in range((rows_x + 2) // 3):
            along_x(i, 0)
        inner = slice(2, rows_x + 2)
        vy[:, YA - 1 : YA, :] = vy[:, YA - 1 : YA, :] - 0.25 * inv_y[0] * (
            p_ext[s, inner, YA : YA + 1, :] - p_ext[s, inner, YA - 2 : YA - 1, :]
        )
        end_y = YA + rows_y
        vy[:, end_y : end_y + 1, :] = vy[:, end_y : end_y + 1, :] - 0.25 * inv_y[1] * (
            p_ext[s, inner, end_y + 1 : end_y + 2, :] - p_ext[s, inner, end_y - 1 : end_y, :]
        )
        chunk = 4
        for i in range(0, rows_x, chunk):
            at = pl.ds(i, chunk)
            at_p = pl.ds(i + 2, chunk)
            here = p_ext[s, at_p, y_in, :]
            rho = inv[pl.ds(i + 1, chunk)]
            vy[at, y_in, :] = vy[at, y_in, :] - 0.25 * rho * (
                p_ext[s, at_p, pl.ds(YA + 1, rows_y), :] - p_ext[s, at_p, pl.ds(YA - 1, rows_y), :]
            )
            halo_p = fill_p[at]
            above_p = pltpu.roll(jnp.where(row_lane == 0, halo_p, here), depth - 1, 2)
            below_p = pltpu.roll(jnp.where(row_lane == depth - 1, halo_p, here), 1, 2)
            vz[at] = vz[at] - 0.5 * rho * (up * above_p + mid * here + low * below_p)
        if last:
            v_out[0] = vx[1 : rows_x + 1]
            v_out[1] = vy[:, YA : YA + rows_y, :]
            v_out[2] = vz[...]
            owner_sums()
        for i in range(0, rows_x, chunk):
            at = pl.ds(i, chunk)
            at_p = pl.ds(i + 2, chunk)
            w = vz[at]
            halo_v = fill_v[at]
            above_v = pltpu.roll(jnp.where(row_lane == 0, halo_v, w), depth - 1, 2)
            below_v = pltpu.roll(jnp.where(row_lane == depth - 1, halo_v, w), 1, 2)
            spread = (
                0.5 * (vx[pl.ds(i + 2, chunk)] - vx[at])
                + 0.5 * (vy[at, pl.ds(YA + 1, rows_y), :] - vy[at, pl.ds(YA - 1, rows_y), :])
                + (up * above_v + mid * w + low * below_v)
            )
            added = jnp.where(row_lane == 0, pltpu.roll(source[at], (depth - s) % depth, 2), 0.0)
            new = p_ext[s, at_p, y_in, :] - 0.5 * bulk[at] * spread + added
            if last:
                p_out[at] = new
            else:
                p_ext[s + 1, at_p, y_in, :] = new

    for load in loads:
        load.wait()
    zi_send[0] = packed(lambda x, y: vz[x, pl.ds(y, 8), :])
    zi_send[1] = packed(lambda x, y: inv[1 + x, pl.ds(y, 8), :])
    for side, y in ((0, 0), (1, rows_y - 1)):
        yi_send[side, :, 0:1, :] = vy[:, YA + y : YA + y + 1, :]
        yi_send[side, :, 1:2, :] = inv[1 : rows_x + 1, y : y + 1, :]
    count = sum(has[f].astype(jnp.int32) for f in faces)
    count = count + jnp.where(at_sea, tiles - 1 + n_z - 1, 0)
    pl.semaphore_wait(barrier, count)
    send(0)
    for f in faces:

        @pl.when(has[f])
        def _(f=f):
            for copy in init_copies(*f, other[f]):
                copy.start()

    cell_x = gx_ref[...] - me[0] * rows_x
    cell_y = gy_ref[...] - me[1] * rows_y
    inside = (cell_x >= 0) & (cell_x < rows_x) & (cell_y >= 0) & (cell_y < rows_y)
    cell = jnp.where(inside, cell_x * rows_y + cell_y, -1)
    gauges = cell.shape[1]
    hot = (lax.broadcasted_iota(jnp.int32, (cells, gauges), 0) == cell).astype(F32)
    scaled = misfit_ref[...] * jnp.where(me[2] == 0, 0.5, 0.0).astype(F32)
    scaled = jnp.concatenate([scaled, jnp.zeros((depth - ITERS, gauges), F32)], axis=0)
    planes = lax.dot_general(hot, scaled, NT, precision=HIGHEST, preferred_element_type=F32)
    source[...] = planes.reshape(rows_x, rows_y, depth)

    nodes = patch_ref.shape[-1]
    patches = slot_ref.shape[1]
    per = patches // tiles
    shift = per.bit_length() - 1
    assert per == 1 << shift and per == 128
    block = min(patches, 1024)
    patch = patch_ref[...].reshape(1, nodes)
    slot_parts = jnp.zeros((8, nodes), F32)
    first_row = lax.broadcasted_iota(jnp.int32, (8, block), 0) == 0
    for at in range(0, patches, block):
        slots = slot_ref[:, at : at + block]
        table = jnp.where(first_row, slots >> shift, slots & (per - 1)).astype(F32)
        hot = lax.broadcasted_iota(jnp.int32, (block, nodes), 0) + at == patch
        slot_parts = slot_parts + jnp.dot(
            table.astype(jnp.bfloat16),
            hot.astype(F32).astype(jnp.bfloat16),
            preferred_element_type=F32,
        )
    slot = (slot_parts[0:1] * per + slot_parts[1:2]).astype(jnp.int32)
    for at in range(0, patches, block):
        hot = lax.broadcasted_iota(jnp.int32, (block, nodes), 0) + at == slot
        slot_hot[pl.ds(at, block), :] = hot.astype(F32).astype(jnp.bfloat16)
    node = lax.broadcasted_iota(jnp.int32, (depth, nodes), 1)
    spread_hot[...] = (
        lax.broadcasted_iota(jnp.int32, (depth, nodes), 0) == 4 * (node >> 3) + 2
    ).astype(F32)

    def slip_copy(o_x, o_y, source_tile):
        return pltpu.make_async_remote_copy(
            src_ref=part.at[o_x * n_y + o_y],
            dst_ref=got.at[source_tile],
            send_sem=slip_send.at[o_x * n_y + o_y],
            recv_sem=slip_recv.at[source_tile],
            device_id=(o_x, o_y, me[2]),
            device_id_type=MESH_ID,
        )

    def depth_copy(c, slot):
        return pltpu.make_async_remote_copy(
            src_ref=total,
            dst_ref=got_all.at[slot],
            send_sem=depth_send.at[c],
            recv_sem=depth_recv.at[slot],
            device_id=(me[0], me[1], c),
            device_id_type=MESH_ID,
        )

    my_slot = jnp.where(me[2] >= root, 1, 0)

    def finish_sea(sea):
        @pl.when(at_sea)
        def _():
            mine = 0.5 * jnp.where(me[2] == root, sea, pltpu.roll(sea, 1, 1))
            values = jnp.dot(mine, spread_hot[...], precision=HIGHEST, preferred_element_type=F32)
            sub = lax.broadcasted_iota(jnp.int32, (8, nodes), 0)
            col = lax.broadcasted_iota(jnp.int32, (8, nodes), 1)
            row = jnp.sum(jnp.where((col & 7) == sub, values, 0.0), axis=0, keepdims=True)
            row = row * weight_ref[...].reshape(1, nodes)
            high = row.astype(jnp.bfloat16).astype(F32)
            rest = row - high
            middle = rest.astype(jnp.bfloat16).astype(F32)
            lowest = rest - middle
            split = jnp.where(
                sub == 0, high, jnp.where(sub == 1, middle, jnp.where(sub == 2, lowest, 0.0))
            ).astype(jnp.bfloat16)
            for at in range(0, patches, block):
                sums = lax.dot_general(
                    split, slot_hot[pl.ds(at, block), :], NT, preferred_element_type=F32
                )
                sums = jnp.sum(sums, axis=0, keepdims=True)
                for o in range(block // per):
                    part[at // per + o] = sums[:, o * per : (o + 1) * per]
            got[tile] = part[tile]
            each_tile(lambda o_x, o_y: slip_copy(o_x, o_y, tile).start())

    def owner_sums():
        @pl.when(at_sea)
        def _():
            each_tile(lambda o_x, o_y: slip_copy(o_x, o_y, o_x * n_y + o_y).wait_recv())
            total[...] = jnp.sum(got[...], axis=0)
            got_all[my_slot] = total[...]
            for c in range(n_z):

                @pl.when(me[2] != c)
                def _(c=c):
                    depth_copy(c, my_slot).start()

    for f in faces:

        @pl.when(has[f])
        def _(f=f):
            for copy in init_copies(f[0], 1 - f[1], other[f]):
                copy.wait_recv()

    for side, y in ((0, YA - 1), (1, YA + rows_y)):
        vy[:, y : y + 1, :] = yi_recv[side, :, 0:1, :]
        inv_y[side] = yi_recv[side, :, 1:2, :]
    kept = (quad == 1) | (quad == 2)
    vz_edge[...] = jnp.where(
        kept, jnp.where(quad == 1, zi_recv[0, 0], zi_recv[1, 0]), 0.0
    )
    pack_edge[...] = jnp.where(
        kept, jnp.where(quad == 1, zi_recv[0, 1], zi_recv[1, 1]), 0.0
    )

    receive(0)
    sea = z_send[0]
    update(0, False)
    for s in range(1, ITERS):
        send(s)
        sea = sea + z_send[s]
        if s == ITERS - 1:
            finish_sea(sea)
        receive(s)
        update(s, s == ITERS - 1)

    for slot_at, c in ((0, root - 1), (1, root)):

        @pl.when(me[2] != c)
        def _(slot_at=slot_at):
            depth_copy(0, slot_at).wait_recv()

    sums = got_all[0] + got_all[1]
    piece = per // n_z
    picked = sums[:, 0:piece]
    for c in range(1, n_z):
        picked = jnp.where(me[2] == c, sums[:, c * piece : (c + 1) * piece], picked)
    slip_out[...] = picked

    for f in faces:

        @pl.when(has[f])
        def _(f=f):
            for copy in init_copies(*f, other[f]):
                copy.wait_send()
            for s in range(ITERS):
                step_copies[f[0]](s, f[1], other[f]).wait_send()

    @pl.when(at_sea)
    def _():
        each_tile(lambda o_x, o_y: slip_copy(o_x, o_y, tile).wait_send())
        for c in range(n_z):

            @pl.when(me[2] != c)
            def _(c=c):
                depth_copy(c, my_slot).wait_send()


def local(sizes, pressure, velocity, inv_density, bulk, node_weight, node_patch, patch_slot,
          gauge_x, gauge_y, gauge_misfit):
    rows_x, rows_y, depth = pressure.shape
    n_x, n_y, n_z = sizes
    tiles = n_x * n_y
    nodes = node_patch.shape[-1]
    patches = patch_slot.shape[0]
    per = patches // tiles
    wide_y = rows_y + 2 * YA
    box = (rows_x, rows_y, depth)
    vmem = pl.BlockSpec(memory_space=pltpu.VMEM)
    hbm = pl.BlockSpec(memory_space=pltpu.HBM)
    gauges = gauge_x.shape[0]
    scratch = [
        pltpu.VMEM((1, 1, nodes), F32),
        pltpu.VMEM((1, 1, nodes), jnp.int32),
        pltpu.VMEM((1, patches), jnp.int32),
        pltpu.VMEM((1, gauges), jnp.int32),
        pltpu.VMEM((1, gauges), jnp.int32),
        pltpu.VMEM((ITERS, gauges), F32),
        pltpu.VMEM((ITERS, rows_x + 4, wide_y, depth), F32),
        pltpu.VMEM((rows_x + 2, rows_y, depth), F32),
        pltpu.VMEM((rows_x, wide_y, depth), F32),
        pltpu.VMEM(box, F32),
        pltpu.VMEM((rows_x + 2, rows_y, depth), F32),
        pltpu.VMEM((2, rows_x, 1, depth), F32),
        pltpu.VMEM(box, F32),
        pltpu.VMEM((8, depth), F32),
        pltpu.VMEM((8, depth), F32),
        pltpu.VMEM(box, F32),
        pltpu.VMEM(box, F32),
        pltpu.VMEM((ITERS, 2, rows_x, 2, depth), F32),
        pltpu.VMEM((ITERS, 2, rows_x, 2, depth), F32),
        pltpu.VMEM((ITERS, 8, depth), F32),
        pltpu.VMEM((ITERS, 2, 8, depth), F32),
        pltpu.VMEM((2, rows_x, 2, depth), F32),
        pltpu.VMEM((2, rows_x, 2, depth), F32),
        pltpu.VMEM((2, 8, depth), F32),
        pltpu.VMEM((2, 2, 8, depth), F32),
        pltpu.VMEM(box, F32),
        pltpu.VMEM((patches, nodes), jnp.bfloat16),
        pltpu.VMEM((depth, nodes), F32),
        pltpu.VMEM((tiles, 1, per), F32),
        pltpu.VMEM((tiles, 1, per), F32),
        pltpu.VMEM((1, per), F32),
        pltpu.VMEM((2, 1, per), F32),
        pltpu.SemaphoreType.DMA((12,)),
        pltpu.SemaphoreType.DMA((ITERS, 6)),
        pltpu.SemaphoreType.DMA((ITERS, 6)),
        pltpu.SemaphoreType.DMA((8,)),
        pltpu.SemaphoreType.DMA((8,)),
        pltpu.SemaphoreType.DMA((tiles,)),
        pltpu.SemaphoreType.DMA((tiles,)),
        pltpu.SemaphoreType.DMA((n_z,)),
        pltpu.SemaphoreType.DMA((2,)),
    ]
    p_new, v_new, slip = pl.pallas_call(
        functools.partial(kernel, sizes),
        out_shape=[
            jax.ShapeDtypeStruct(box, F32),
            jax.ShapeDtypeStruct((3,) + box, F32),
            jax.ShapeDtypeStruct((1, per // n_z), F32),
        ],
        in_specs=[hbm] * 10,
        out_specs=[vmem] * 3,
        scratch_shapes=scratch,
        compiler_params=pltpu.CompilerParams(
            collective_id=0, has_side_effects=True, vmem_limit_bytes=64 * 1024 * 1024 - 64 * 1024
        ),
    )(
        pressure,
        velocity,
        inv_density,
        bulk,
        node_weight,
        node_patch,
        patch_slot.reshape(1, patches),
        gauge_x.reshape(1, -1),
        gauge_y.reshape(1, -1),
        gauge_misfit,
    )
    return p_new, v_new, slip.reshape(per // n_z)


def solution(mesh):
    placed = (
        P("gx", "gy", "gz"),
        P(None, "gx", "gy", "gz"),
        P("gx", "gy", "gz"),
        P("gx", "gy", "gz"),
        P("gx", "gy", None),
        P("gx", "gy", None),
        P(),
        P(),
        P(),
        P(),
    )
    sizes = tuple(mesh.shape[a] for a in AXES)
    return jax.shard_map(
        functools.partial(local, sizes),
        mesh=mesh,
        in_specs=placed,
        out_specs=(P("gx", "gy", "gz"), P(None, "gx", "gy", "gz"), P(("gx", "gy", "gz"))),
        check_vma=False,
    )
```

```python
import functools

import jax
import jax.numpy as jnp
from jax import lax
from jax.experimental import pallas as pl
from jax.experimental.pallas import tpu as pltpu
from jax.sharding import PartitionSpec as P

ITERS = 4
MESH_ID = pl.DeviceIdType.MESH
AXES = ("gx", "gy", "gz")
YA = 8
F32 = jnp.float32
HIGHEST = lax.Precision.HIGHEST
NT = (((1,), (1,)), ((), ()))


def kernel(
    sizes,
    p_in,
    v_in,
    d_in,
    b_in,
    weight_in,
    patch_in,
    slot_in,
    gx_in,
    gy_in,
    misfit_in,
    p_out,
    v_out,
    slip_out,
    weight_ref,
    patch_ref,
    slot_ref,
    gx_ref,
    gy_ref,
    misfit_ref,
    p_ext,
    vx,
    vy,
    vz,
    inv,
    inv_y,
    bulk,
    pack_edge,
    vz_edge,
    fill_p,
    fill_v,
    y_send,
    y_recv,
    z_send,
    z_recv,
    yi_send,
    yi_recv,
    zi_send,
    zi_recv,
    source,
    slot_hot,
    spread_hot,
    part,
    got,
    total,
    got_all,
    load_sem,
    send_sem,
    recv_sem,
    init_send,
    init_recv,
    slip_send,
    slip_recv,
    depth_send,
    depth_recv,
):
    n_x, n_y, n_z = sizes
    rows_x, rows_y, depth = p_in.shape
    cells = rows_x * rows_y
    halves = rows_y // 8
    me = [lax.axis_index(a) for a in AXES]
    tiles = n_x * n_y
    tile = me[0] * n_y + me[1]
    root = n_z // 2
    has = {}
    other = {}
    for a in range(3):
        has[a, 0] = me[a] > 0
        has[a, 1] = me[a] < sizes[a] - 1
        for side in (0, 1):
            to = list(me)
            to[a] = me[a] + (2 * side - 1)
            other[a, side] = tuple(to)
    faces = [(a, side) for a in range(3) for side in (0, 1) if sizes[a] > 1]

    y_in = pl.ds(YA, rows_y)
    x_in = pl.ds(2, rows_x)
    loads = [
        pltpu.make_async_copy(p_in, p_ext.at[0, x_in, y_in], load_sem.at[0]),
        pltpu.make_async_copy(d_in, inv.at[pl.ds(1, rows_x)], load_sem.at[1]),
        pltpu.make_async_copy(v_in.at[2], vz, load_sem.at[2]),
        pltpu.make_async_copy(v_in.at[1], vy.at[:, y_in], load_sem.at[3]),
        pltpu.make_async_copy(v_in.at[0], vx.at[pl.ds(1, rows_x)], load_sem.at[4]),
        pltpu.make_async_copy(b_in, bulk, load_sem.at[5]),
        pltpu.make_async_copy(weight_in, weight_ref, load_sem.at[6]),
        pltpu.make_async_copy(patch_in, patch_ref, load_sem.at[7]),
        pltpu.make_async_copy(slot_in, slot_ref, load_sem.at[8]),
        pltpu.make_async_copy(gx_in, gx_ref, load_sem.at[9]),
        pltpu.make_async_copy(gy_in, gy_ref, load_sem.at[10]),
        pltpu.make_async_copy(misfit_in, misfit_ref, load_sem.at[11]),
    ]
    for load in loads:
        load.start()

    barrier = pltpu.get_barrier_semaphore()
    for f in faces:

        @pl.when(has[f])
        def _(f=f):
            pl.semaphore_signal(barrier, inc=1, device_id=other[f], device_id_type=MESH_ID)

    at_sea = (me[2] == root) | (me[2] == root - 1)

    def each_tile(act):
        def one(o_x, o_y):
            @pl.when((o_x != me[0]) | (o_y != me[1]))
            def _():
                act(o_x, o_y)

        if tiles <= 8:
            for o in range(tiles):
                one(o // n_y, o % n_y)
        else:

            def row(o_x, _):
                def column(o_y, _):
                    one(o_x, o_y)
                    return 0

                return lax.fori_loop(0, n_y, column, 0)

            lax.fori_loop(0, n_x, row, 0)

    def greet(o_x, o_y):
        pl.semaphore_signal(
            barrier, inc=1, device_id=(o_x, o_y, me[2]), device_id_type=MESH_ID
        )

    @pl.when(at_sea)
    def _():
        each_tile(greet)

    for c in (root - 1, root):

        @pl.when(me[2] != c)
        def _(c=c):
            pl.semaphore_signal(
                barrier, inc=1, device_id=(me[0], me[1], c), device_id_type=MESH_ID
            )

    for side in (0, 1):

        @pl.when(jnp.logical_not(has[0, side]))
        def _(side=side):
            at = 0 if side == 0 else rows_x + 2
            p_ext[:, pl.ds(at, 2), :, :] = jnp.zeros_like(p_ext[:, pl.ds(at, 2), :, :])
            one = 0 if side == 0 else rows_x + 1
            vx[one] = jnp.zeros_like(vx[one])
            inv[one] = jnp.zeros_like(inv[one])

        @pl.when(jnp.logical_not(has[1, side]))
        def _(side=side):
            y_recv[:, side] = jnp.zeros_like(y_recv[:, side])
            yi_recv[side] = jnp.zeros_like(yi_recv[side])

        @pl.when(jnp.logical_not(has[2, side]))
        def _(side=side):
            z_recv[:, side] = jnp.zeros_like(z_recv[:, side])
            zi_recv[side] = jnp.zeros_like(zi_recv[side])

    lane = lax.broadcasted_iota(jnp.int32, (8, depth), 1)
    quad = lane & 3
    group = lane >> 2

    def packed(read):
        q = jnp.zeros((8, depth), F32)
        for j in range(rows_x * halves):
            rolled = pltpu.roll(read(j // halves, (j % halves) * 8), (4 * j + 2) % depth, 1)
            q = jnp.where(group == j, rolled, q)
        return q

    def unpack(tile_value, ref):
        for j in range(rows_x * halves):
            ref[j // halves, pl.ds((j % halves) * 8, 8), :] = pltpu.roll(
                tile_value, (-(4 * j + 2)) % depth, 1
            )

    def coefs(level):
        first = root * depth
        last_ocean = level == first - 1
        crust = level == first
        up = jnp.where(crust, 1.0, 0.5).astype(F32)
        mid = jnp.where(last_ocean, 0.5, jnp.where(crust, -1.5, 0.0)).astype(F32)
        low = jnp.where(last_ocean, -1.0, jnp.where(crust, 0.5, -0.5)).astype(F32)
        return up, mid, low

    row_lane = lax.broadcasted_iota(jnp.int32, (1, 1, depth), 2)
    up, mid, low = coefs(me[2] * depth + row_lane)
    up_e, mid_e, low_e = coefs(
        jnp.where(quad == 1, me[2] * depth - 1, (me[2] + 1) * depth)
    )

    def copy_x(s, side, to):
        src, dst = (2, rows_x + 2) if side == 0 else (rows_x, 0)
        return pltpu.make_async_remote_copy(
            src_ref=p_ext.at[s, pl.ds(src, 2), y_in],
            dst_ref=p_ext.at[s, pl.ds(dst, 2), y_in],
            send_sem=send_sem.at[s, side],
            recv_sem=recv_sem.at[s, 1 - side],
            device_id=to,
            device_id_type=MESH_ID,
        )

    def copy_y(s, side, to):
        return pltpu.make_async_remote_copy(
            src_ref=y_send.at[s, side],
            dst_ref=y_recv.at[s, 1 - side],
            send_sem=send_sem.at[s, 2 + side],
            recv_sem=recv_sem.at[s, 3 - side],
            device_id=to,
            device_id_type=MESH_ID,
        )

    def copy_z(s, side, to):
        return pltpu.make_async_remote_copy(
            src_ref=z_send.at[s],
            dst_ref=z_recv.at[s, 1 - side],
            send_sem=send_sem.at[s, 4 + side],
            recv_sem=recv_sem.at[s, 5 - side],
            device_id=to,
            device_id_type=MESH_ID,
        )

    step_copies = {0: copy_x, 1: copy_y, 2: copy_z}

    def init_copy(src, dst, to, n, back):
        return pltpu.make_async_remote_copy(
            src_ref=src,
            dst_ref=dst,
            send_sem=init_send.at[n],
            recv_sem=init_recv.at[back],
            device_id=to,
            device_id_type=MESH_ID,
        )

    def init_copies(a, side, to):
        if a == 0:
            src, dst = (0, rows_x + 1) if side == 0 else (rows_x - 1, 0)
            return [
                init_copy(
                    v_in.at[0, pl.ds(src, 1)], vx.at[pl.ds(dst, 1)], to, side, 1 - side
                ),
                init_copy(
                    inv.at[pl.ds(src + 1, 1)], inv.at[pl.ds(dst, 1)], to, 6 + side, 7 - side
                ),
            ]
        if a == 1:
            return [init_copy(yi_send.at[side], yi_recv.at[1 - side], to, 2 + side, 3 - side)]
        return [init_copy(zi_send, zi_recv.at[1 - side], to, 4 + side, 5 - side)]

    def send(s):
        z_send[s] = packed(lambda x, y: p_ext[s, 2 + x, pl.ds(YA + y, 8), :])
        y_send[s, 0] = p_ext[s, 2 : rows_x + 2, YA : YA + 2, :]
        y_send[s, 1] = p_ext[s, 2 : rows_x + 2, YA + rows_y - 2 : YA + rows_y, :]
        for f in faces:

            @pl.when(has[f])
            def _(f=f):
                step_copies[f[0]](s, f[1], other[f]).start()

    def receive(s):
        for f in faces:

            @pl.when(has[f])
            def _(f=f):
                step_copies[f[0]](s, 1 - f[1], other[f]).wait_recv()

        p_ext[s, 2 : rows_x + 2, YA - 2 : YA, :] = y_recv[s, 0]
        p_ext[s, 2 : rows_x + 2, YA + rows_y : YA + rows_y + 2, :] = y_recv[s, 1]

    def update(s, last):
        own = z_send[s]
        halo = jnp.where(quad < 2, z_recv[s, 0], z_recv[s, 1])
        above = pltpu.roll(jnp.where(quad == 2, own, halo), depth - 1, 1)
        below = pltpu.roll(jnp.where(quad == 1, own, halo), 1, 1)
        edge = vz_edge[...] - 0.5 * pack_edge[...] * (
            up_e * above + mid_e * halo + low_e * below
        )
        vz_edge[...] = edge
        unpack(halo, fill_p)
        unpack(edge, fill_v)

        def along_x(i, _):
            at = pl.ds(i * 3, 3)
            ahead = p_ext[s, pl.ds(i * 3 + 2, 3), y_in, :]
            behind = p_ext[s, pl.ds(i * 3, 3), y_in, :]
            vx[at] = vx[at] - 0.25 * inv[at] * (ahead - behind)
            return 0

        for i in range((rows_x + 2) // 3):
            along_x(i, 0)
        inner = slice(2, rows_x + 2)
        vy[:, YA - 1 : YA, :] = vy[:, YA - 1 : YA, :] - 0.25 * inv_y[0] * (
            p_ext[s, inner, YA : YA + 1, :] - p_ext[s, inner, YA - 2 : YA - 1, :]
        )
        end_y = YA + rows_y
        vy[:, end_y : end_y + 1, :] = vy[:, end_y : end_y + 1, :] - 0.25 * inv_y[1] * (
            p_ext[s, inner, end_y + 1 : end_y + 2, :] - p_ext[s, inner, end_y - 1 : end_y, :]
        )
        chunk = 4
        for i in range(0, rows_x, chunk):
            at = pl.ds(i, chunk)
            at_p = pl.ds(i + 2, chunk)
            here = p_ext[s, at_p, y_in, :]
            rho = inv[pl.ds(i + 1, chunk)]
            vy[at, y_in, :] = vy[at, y_in, :] - 0.25 * rho * (
                p_ext[s, at_p, pl.ds(YA + 1, rows_y), :] - p_ext[s, at_p, pl.ds(YA - 1, rows_y), :]
            )
            halo_p = fill_p[at]
            above_p = pltpu.roll(jnp.where(row_lane == 0, halo_p, here), depth - 1, 2)
            below_p = pltpu.roll(jnp.where(row_lane == depth - 1, halo_p, here), 1, 2)
            vz[at] = vz[at] - 0.5 * rho * (up * above_p + mid * here + low * below_p)
        if last:
            v_out[0] = vx[1 : rows_x + 1]
            v_out[1] = vy[:, YA : YA + rows_y, :]
            v_out[2] = vz[...]
            owner_sums()
        for i in range(0, rows_x, chunk):
            at = pl.ds(i, chunk)
            at_p = pl.ds(i + 2, chunk)
            w = vz[at]
            halo_v = fill_v[at]
            above_v = pltpu.roll(jnp.where(row_lane == 0, halo_v, w), depth - 1, 2)
            below_v = pltpu.roll(jnp.where(row_lane == depth - 1, halo_v, w), 1, 2)
            spread = (
                0.5 * (vx[pl.ds(i + 2, chunk)] - vx[at])
                + 0.5 * (vy[at, pl.ds(YA + 1, rows_y), :] - vy[at, pl.ds(YA - 1, rows_y), :])
                + (up * above_v + mid * w + low * below_v)
            )
            added = jnp.where(row_lane == 0, pltpu.roll(source[at], (depth - s) % depth, 2), 0.0)
            new = p_ext[s, at_p, y_in, :] - 0.5 * bulk[at] * spread + added
            if last:
                p_out[at] = new
            else:
                p_ext[s + 1, at_p, y_in, :] = new

    for load in loads:
        load.wait()
    zi_send[0] = packed(lambda x, y: vz[x, pl.ds(y, 8), :])
    zi_send[1] = packed(lambda x, y: inv[1 + x, pl.ds(y, 8), :])
    for side, y in ((0, 0), (1, rows_y - 1)):
        yi_send[side, :, 0:1, :] = vy[:, YA + y : YA + y + 1, :]
        yi_send[side, :, 1:2, :] = inv[1 : rows_x + 1, y : y + 1, :]
    count = sum(has[f].astype(jnp.int32) for f in faces)
    count = count + jnp.where(at_sea, tiles - 1 + n_z - 1, 0)
    pl.semaphore_wait(barrier, count)
    send(0)
    for f in faces:

        @pl.when(has[f])
        def _(f=f):
            for copy in init_copies(*f, other[f]):
                copy.start()

    cell_x = gx_ref[...] - me[0] * rows_x
    cell_y = gy_ref[...] - me[1] * rows_y
    inside = (cell_x >= 0) & (cell_x < rows_x) & (cell_y >= 0) & (cell_y < rows_y)
    cell = jnp.where(inside, cell_x * rows_y + cell_y, -1)
    gauges = cell.shape[1]
    hot = (lax.broadcasted_iota(jnp.int32, (cells, gauges), 0) == cell).astype(F32)
    scaled = misfit_ref[...] * jnp.where(me[2] == 0, 0.5, 0.0).astype(F32)
    scaled = jnp.concatenate([scaled, jnp.zeros((depth - ITERS, gauges), F32)], axis=0)
    planes = lax.dot_general(hot, scaled, NT, precision=HIGHEST, preferred_element_type=F32)
    source[...] = planes.reshape(rows_x, rows_y, depth)

    nodes = patch_ref.shape[-1]
    patches = slot_ref.shape[1]
    per = patches // tiles
    shift = per.bit_length() - 1
    assert per == 1 << shift and per == 128
    block = min(patches, 1024)
    patch = patch_ref[...].reshape(1, nodes)
    slot_parts = jnp.zeros((8, nodes), F32)
    first_row = lax.broadcasted_iota(jnp.int32, (8, block), 0) == 0
    for at in range(0, patches, block):
        slots = slot_ref[:, at : at + block]
        table = jnp.where(first_row, slots >> shift, slots & (per - 1)).astype(F32)
        hot = lax.broadcasted_iota(jnp.int32, (block, nodes), 0) + at == patch
        slot_parts = slot_parts + jnp.dot(
            table.astype(jnp.bfloat16),
            hot.astype(F32).astype(jnp.bfloat16),
            preferred_element_type=F32,
        )
    slot = (slot_parts[0:1] * per + slot_parts[1:2]).astype(jnp.int32)
    for at in range(0, patches, block):
        hot = lax.broadcasted_iota(jnp.int32, (block, nodes), 0) + at == slot
        slot_hot[pl.ds(at, block), :] = hot.astype(F32).astype(jnp.bfloat16)
    node = lax.broadcasted_iota(jnp.int32, (depth, nodes), 1)
    spread_hot[...] = (
        lax.broadcasted_iota(jnp.int32, (depth, nodes), 0) == 4 * (node >> 3) + 2
    ).astype(F32)

    def slip_copy(o_x, o_y, source_tile):
        return pltpu.make_async_remote_copy(
            src_ref=part.at[o_x * n_y + o_y],
            dst_ref=got.at[source_tile],
            send_sem=slip_send.at[o_x * n_y + o_y],
            recv_sem=slip_recv.at[source_tile],
            device_id=(o_x, o_y, me[2]),
            device_id_type=MESH_ID,
        )

    def depth_copy(c, slot):
        return pltpu.make_async_remote_copy(
            src_ref=total,
            dst_ref=got_all.at[slot],
            send_sem=depth_send.at[c],
            recv_sem=depth_recv.at[slot],
            device_id=(me[0], me[1], c),
            device_id_type=MESH_ID,
        )

    my_slot = jnp.where(me[2] >= root, 1, 0)

    def finish_sea(sea):
        @pl.when(at_sea)
        def _():
            mine = 0.5 * jnp.where(me[2] == root, sea, pltpu.roll(sea, 1, 1))
            values = jnp.dot(mine, spread_hot[...], precision=HIGHEST, preferred_element_type=F32)
            sub = lax.broadcasted_iota(jnp.int32, (8, nodes), 0)
            col = lax.broadcasted_iota(jnp.int32, (8, nodes), 1)
            row = jnp.sum(jnp.where((col & 7) == sub, values, 0.0), axis=0, keepdims=True)
            row = row * weight_ref[...].reshape(1, nodes)
            high = row.astype(jnp.bfloat16).astype(F32)
            rest = row - high
            middle = rest.astype(jnp.bfloat16).astype(F32)
            lowest = rest - middle
            split = jnp.where(
                sub == 0, high, jnp.where(sub == 1, middle, jnp.where(sub == 2, lowest, 0.0))
            ).astype(jnp.bfloat16)
            for at in range(0, patches, block):
                sums = lax.dot_general(
                    split, slot_hot[pl.ds(at, block), :], NT, preferred_element_type=F32
                )
                sums = jnp.sum(sums, axis=0, keepdims=True)
                for o in range(block // per):
                    part[at // per + o] = sums[:, o * per : (o + 1) * per]
            got[tile] = part[tile]
            each_tile(lambda o_x, o_y: slip_copy(o_x, o_y, tile).start())

    def owner_sums():
        @pl.when(at_sea)
        def _():
            each_tile(lambda o_x, o_y: slip_copy(o_x, o_y, o_x * n_y + o_y).wait_recv())
            total[...] = jnp.sum(got[...], axis=0)
            got_all[my_slot] = total[...]
            for c in range(n_z):

                @pl.when(me[2] != c)
                def _(c=c):
                    depth_copy(c, my_slot).start()

    for f in faces:

        @pl.when(has[f])
        def _(f=f):
            for copy in init_copies(f[0], 1 - f[1], other[f]):
                copy.wait_recv()

    for side, y in ((0, YA - 1), (1, YA + rows_y)):
        vy[:, y : y + 1, :] = yi_recv[side, :, 0:1, :]
        inv_y[side] = yi_recv[side, :, 1:2, :]
    kept = (quad == 1) | (quad == 2)
    vz_edge[...] = jnp.where(
        kept, jnp.where(quad == 1, zi_recv[0, 0], zi_recv[1, 0]), 0.0
    )
    pack_edge[...] = jnp.where(
        kept, jnp.where(quad == 1, zi_recv[0, 1], zi_recv[1, 1]), 0.0
    )

    receive(0)
    sea = z_send[0]
    update(0, False)
    for s in range(1, ITERS):
        send(s)
        sea = sea + z_send[s]
        if s == ITERS - 1:
            finish_sea(sea)
        receive(s)
        update(s, s == ITERS - 1)

    for slot_at, c in ((0, root - 1), (1, root)):

        @pl.when(me[2] != c)
        def _(slot_at=slot_at):
            depth_copy(0, slot_at).wait_recv()

    sums = got_all[0] + got_all[1]
    piece = per // n_z
    picked = sums[:, 0:piece]
    for c in range(1, n_z):
        picked = jnp.where(me[2] == c, sums[:, c * piece : (c + 1) * piece], picked)
    slip_out[...] = picked

    for f in faces:

        @pl.when(has[f])
        def _(f=f):
            for copy in init_copies(*f, other[f]):
                copy.wait_send()
            for s in range(ITERS):
                step_copies[f[0]](s, f[1], other[f]).wait_send()

    @pl.when(at_sea)
    def _():
        each_tile(lambda o_x, o_y: slip_copy(o_x, o_y, tile).wait_send())
        for c in range(n_z):

            @pl.when(me[2] != c)
            def _(c=c):
                depth_copy(c, my_slot).wait_send()


def write_out(p_in, v_in, slip_in, p_out, v_out, slip_out, sem):
    copies = [
        pltpu.make_async_copy(src, dst, sem.at[n])
        for n, (src, dst) in enumerate([(v_in, v_out), (p_in, p_out), (slip_in, slip_out)])
    ]
    for copy in copies:
        copy.start()
    for copy in copies:
        copy.wait()


def local(sizes, pressure, velocity, inv_density, bulk, node_weight, node_patch, patch_slot,
          gauge_x, gauge_y, gauge_misfit):
    rows_x, rows_y, depth = pressure.shape
    n_x, n_y, n_z = sizes
    tiles = n_x * n_y
    nodes = node_patch.shape[-1]
    patches = patch_slot.shape[0]
    per = patches // tiles
    wide_y = rows_y + 2 * YA
    box = (rows_x, rows_y, depth)
    vmem = pl.BlockSpec(memory_space=pltpu.VMEM)
    hbm = pl.BlockSpec(memory_space=pltpu.HBM)
    gauges = gauge_x.shape[0]
    scratch = [
        pltpu.VMEM((1, 1, nodes), F32),
        pltpu.VMEM((1, 1, nodes), jnp.int32),
        pltpu.VMEM((1, patches), jnp.int32),
        pltpu.VMEM((1, gauges), jnp.int32),
        pltpu.VMEM((1, gauges), jnp.int32),
        pltpu.VMEM((ITERS, gauges), F32),
        pltpu.VMEM((ITERS, rows_x + 4, wide_y, depth), F32),
        pltpu.VMEM((rows_x + 2, rows_y, depth), F32),
        pltpu.VMEM((rows_x, wide_y, depth), F32),
        pltpu.VMEM(box, F32),
        pltpu.VMEM((rows_x + 2, rows_y, depth), F32),
        pltpu.VMEM((2, rows_x, 1, depth), F32),
        pltpu.VMEM(box, F32),
        pltpu.VMEM((8, depth), F32),
        pltpu.VMEM((8, depth), F32),
        pltpu.VMEM(box, F32),
        pltpu.VMEM(box, F32),
        pltpu.VMEM((ITERS, 2, rows_x, 2, depth), F32),
        pltpu.VMEM((ITERS, 2, rows_x, 2, depth), F32),
        pltpu.VMEM((ITERS, 8, depth), F32),
        pltpu.VMEM((ITERS, 2, 8, depth), F32),
        pltpu.VMEM((2, rows_x, 2, depth), F32),
        pltpu.VMEM((2, rows_x, 2, depth), F32),
        pltpu.VMEM((2, 8, depth), F32),
        pltpu.VMEM((2, 2, 8, depth), F32),
        pltpu.VMEM(box, F32),
        pltpu.VMEM((patches, nodes), jnp.bfloat16),
        pltpu.VMEM((depth, nodes), F32),
        pltpu.VMEM((tiles, 1, per), F32),
        pltpu.VMEM((tiles, 1, per), F32),
        pltpu.VMEM((1, per), F32),
        pltpu.VMEM((2, 1, per), F32),
        pltpu.SemaphoreType.DMA((12,)),
        pltpu.SemaphoreType.DMA((ITERS, 6)),
        pltpu.SemaphoreType.DMA((ITERS, 6)),
        pltpu.SemaphoreType.DMA((8,)),
        pltpu.SemaphoreType.DMA((8,)),
        pltpu.SemaphoreType.DMA((tiles,)),
        pltpu.SemaphoreType.DMA((tiles,)),
        pltpu.SemaphoreType.DMA((n_z,)),
        pltpu.SemaphoreType.DMA((2,)),
    ]
    colored = [pltpu.VMEM(box, F32), pltpu.VMEM((3,) + box, F32), pltpu.VMEM((1, per // n_z), F32)]
    shapes = [
        jax.ShapeDtypeStruct(box, F32),
        jax.ShapeDtypeStruct((3,) + box, F32),
        jax.ShapeDtypeStruct((1, per // n_z), F32),
    ]
    p_new, v_new, slip = pl.pallas_call(
        functools.partial(kernel, sizes),
        out_shape=colored,
        in_specs=[hbm] * 10,
        out_specs=[vmem] * 3,
        scratch_shapes=scratch,
        compiler_params=pltpu.CompilerParams(
            collective_id=0, has_side_effects=True, vmem_limit_bytes=64 * 1024 * 1024 - 1400 * 1024
        ),
    )(
        pressure,
        velocity,
        inv_density,
        bulk,
        node_weight,
        node_patch,
        patch_slot.reshape(1, patches),
        gauge_x.reshape(1, -1),
        gauge_y.reshape(1, -1),
        gauge_misfit,
    )
    anywhere = pl.BlockSpec(memory_space=pl.ANY)
    p_new, v_new, slip = pl.pallas_call(
        write_out,
        out_shape=shapes,
        in_specs=[anywhere] * 3,
        out_specs=[anywhere] * 3,
        scratch_shapes=[pltpu.SemaphoreType.DMA((3,))],
        compiler_params=pltpu.CompilerParams(vmem_limit_bytes=2 * 1024 * 1024),
    )(p_new, v_new, slip)
    return p_new, v_new, slip.reshape(per // n_z)


def solution(mesh):
    placed = (
        P("gx", "gy", "gz"),
        P(None, "gx", "gy", "gz"),
        P("gx", "gy", "gz"),
        P("gx", "gy", "gz"),
        P("gx", "gy", None),
        P("gx", "gy", None),
        P(),
        P(),
        P(),
        P(),
    )
    sizes = tuple(mesh.shape[a] for a in AXES)
    return jax.shard_map(
        functools.partial(local, sizes),
        mesh=mesh,
        in_specs=placed,
        out_specs=(P("gx", "gy", "gz"), P(None, "gx", "gy", "gz"), P(("gx", "gy", "gz"))),
        check_vma=False,
    )
```

```python
import functools

import jax
import jax.numpy as jnp
from jax import lax
from jax.experimental import pallas as pl
from jax.experimental.pallas import tpu as pltpu
from jax.sharding import PartitionSpec as P

ITERS = 4
MESH_ID = pl.DeviceIdType.MESH
AXES = ("gx", "gy", "gz")
YA = 8
F32 = jnp.float32
NT = (((1,), (1,)), ((), ()))


def kernel(
    sizes,
    p_in,
    v_in,
    d_in,
    b_in,
    weight_in,
    patch_in,
    slot_in,
    gx_in,
    gy_in,
    misfit_in,
    p_out,
    v_out,
    slip_out,
    weight_ref,
    patch_ref,
    slot_ref,
    gx_ref,
    gy_ref,
    misfit_ref,
    p_ext,
    vx,
    vy,
    vz,
    inv,
    inv_y,
    bulk,
    pack_edge,
    vz_edge,
    vy_edge,
    vz_change,
    bulk_pack,
    y_send,
    y_recv,
    z_send,
    z_recv,
    yi_send,
    yi_recv,
    zi_send,
    zi_recv,
    source,
    slot_hot,
    spread_hot,
    part,
    got,
    total,
    got_all,
    load_sem,
    send_sem,
    recv_sem,
    init_send,
    init_recv,
    slip_send,
    slip_recv,
    depth_send,
    depth_recv,
):
    n_x, n_y, n_z = sizes
    rows_x, rows_y, depth = p_in.shape
    cells = rows_x * rows_y
    halves = rows_y // 8
    me = [lax.axis_index(a) for a in AXES]
    tiles = n_x * n_y
    tile = me[0] * n_y + me[1]
    root = n_z // 2
    has = {}
    other = {}
    for a in range(3):
        has[a, 0] = me[a] > 0
        has[a, 1] = me[a] < sizes[a] - 1
        for side in (0, 1):
            to = list(me)
            to[a] = me[a] + (2 * side - 1)
            other[a, side] = tuple(to)
    faces = [(a, side) for a in range(3) for side in (0, 1) if sizes[a] > 1]

    y_in = pl.ds(YA, rows_y)
    x_in = pl.ds(2, rows_x)
    loads = [
        pltpu.make_async_copy(p_in, p_ext.at[0, x_in, y_in], load_sem.at[0]),
        pltpu.make_async_copy(d_in, inv.at[pl.ds(1, rows_x)], load_sem.at[1]),
        pltpu.make_async_copy(v_in.at[2], vz, load_sem.at[2]),
        pltpu.make_async_copy(v_in.at[1], vy.at[:, y_in], load_sem.at[3]),
        pltpu.make_async_copy(v_in.at[0], vx.at[pl.ds(1, rows_x)], load_sem.at[4]),
        pltpu.make_async_copy(b_in, bulk, load_sem.at[5]),
        pltpu.make_async_copy(weight_in, weight_ref, load_sem.at[6]),
        pltpu.make_async_copy(patch_in, patch_ref, load_sem.at[7]),
        pltpu.make_async_copy(slot_in, slot_ref, load_sem.at[8]),
        pltpu.make_async_copy(gx_in, gx_ref, load_sem.at[9]),
        pltpu.make_async_copy(gy_in, gy_ref, load_sem.at[10]),
        pltpu.make_async_copy(misfit_in, misfit_ref, load_sem.at[11]),
    ]
    for load in loads:
        load.start()

    barrier = pltpu.get_barrier_semaphore()
    for f in faces:

        @pl.when(has[f])
        def _(f=f):
            pl.semaphore_signal(barrier, inc=1, device_id=other[f], device_id_type=MESH_ID)

    at_sea = (me[2] == root) | (me[2] == root - 1)

    def each_tile(act):
        def one(o_x, o_y):
            @pl.when((o_x != me[0]) | (o_y != me[1]))
            def _():
                act(o_x, o_y)

        if tiles <= 8:
            for o in range(tiles):
                one(o // n_y, o % n_y)
        else:

            def row(o_x, _):
                def column(o_y, _):
                    one(o_x, o_y)
                    return 0

                return lax.fori_loop(0, n_y, column, 0)

            lax.fori_loop(0, n_x, row, 0)

    def greet(o_x, o_y):
        pl.semaphore_signal(
            barrier, inc=1, device_id=(o_x, o_y, me[2]), device_id_type=MESH_ID
        )

    @pl.when(at_sea)
    def _():
        each_tile(greet)

    for c in (root - 1, root):

        @pl.when(me[2] != c)
        def _(c=c):
            pl.semaphore_signal(
                barrier, inc=1, device_id=(me[0], me[1], c), device_id_type=MESH_ID
            )

    for y in (YA - 1, YA + rows_y):
        zero = jnp.zeros((rows_x, 1, depth), F32)
        vy[:, y : y + 1, :] = zero
        for s in range(ITERS):
            p_ext[s, 2 : rows_x + 2, y : y + 1, :] = zero

    for side in (0, 1):

        @pl.when(jnp.logical_not(has[0, side]))
        def _(side=side):
            at = 0 if side == 0 else rows_x + 2
            p_ext[:, pl.ds(at, 2), :, :] = jnp.zeros_like(p_ext[:, pl.ds(at, 2), :, :])
            one = 0 if side == 0 else rows_x + 1
            vx[one] = jnp.zeros_like(vx[one])
            inv[one] = jnp.zeros_like(inv[one])

        @pl.when(jnp.logical_not(has[1, side]))
        def _(side=side):
            y_recv[:, side] = jnp.zeros_like(y_recv[:, side])
            yi_recv[side] = jnp.zeros_like(yi_recv[side])

        @pl.when(jnp.logical_not(has[2, side]))
        def _(side=side):
            z_recv[:, side] = jnp.zeros_like(z_recv[:, side])
            zi_recv[side] = jnp.zeros_like(zi_recv[side])

    lane = lax.broadcasted_iota(jnp.int32, (8, depth), 1)
    quad = lane & 3
    group = lane >> 2

    def packed(read):
        q = jnp.zeros((8, depth), F32)
        for j in range(rows_x * halves):
            rolled = pltpu.roll(read(j // halves, (j % halves) * 8), (4 * j + 2) % depth, 1)
            q = jnp.where(group == j, rolled, q)
        return q

    def coefs(level):
        first = root * depth
        last_ocean = level == first - 1
        crust = level == first
        up = jnp.where(crust, 1.0, 0.5).astype(F32)
        mid = jnp.where(last_ocean, 0.5, jnp.where(crust, -1.5, 0.0)).astype(F32)
        low = jnp.where(last_ocean, -1.0, jnp.where(crust, 0.5, -0.5)).astype(F32)
        return up, mid, low

    row_lane = lax.broadcasted_iota(jnp.int32, (1, 1, depth), 2)
    up, mid, low = coefs(me[2] * depth + row_lane)
    up_e, mid_e, low_e = coefs(
        jnp.where(quad == 1, me[2] * depth - 1, (me[2] + 1) * depth)
    )

    up_o, mid_o, low_o = coefs(
        me[2] * depth + jnp.where(quad < 2, depth - 2 + quad, quad - 2)
    )

    def copy_x(s, side, to):
        src, dst = (2, rows_x + 2) if side == 0 else (rows_x, 0)
        return pltpu.make_async_remote_copy(
            src_ref=p_ext.at[s, pl.ds(src, 2), y_in],
            dst_ref=p_ext.at[s, pl.ds(dst, 2), y_in],
            send_sem=send_sem.at[s, side],
            recv_sem=recv_sem.at[s, 1 - side],
            device_id=to,
            device_id_type=MESH_ID,
        )

    def copy_y(s, side, to):
        return pltpu.make_async_remote_copy(
            src_ref=y_send.at[s, side],
            dst_ref=y_recv.at[s, 1 - side],
            send_sem=send_sem.at[s, 2 + side],
            recv_sem=recv_sem.at[s, 3 - side],
            device_id=to,
            device_id_type=MESH_ID,
        )

    def copy_z(s, side, to):
        return pltpu.make_async_remote_copy(
            src_ref=z_send.at[s],
            dst_ref=z_recv.at[s, 1 - side],
            send_sem=send_sem.at[s, 4 + side],
            recv_sem=recv_sem.at[s, 5 - side],
            device_id=to,
            device_id_type=MESH_ID,
        )

    step_copies = {0: copy_x, 1: copy_y, 2: copy_z}

    def init_copy(src, dst, to, n, back):
        return pltpu.make_async_remote_copy(
            src_ref=src,
            dst_ref=dst,
            send_sem=init_send.at[n],
            recv_sem=init_recv.at[back],
            device_id=to,
            device_id_type=MESH_ID,
        )

    def init_copies(a, side, to):
        if a == 0:
            src, dst = (0, rows_x + 1) if side == 0 else (rows_x - 1, 0)
            return [
                init_copy(
                    v_in.at[0, pl.ds(src, 1)], vx.at[pl.ds(dst, 1)], to, side, 1 - side
                ),
                init_copy(
                    inv.at[pl.ds(src + 1, 1)], inv.at[pl.ds(dst, 1)], to, 6 + side, 7 - side
                ),
            ]
        if a == 1:
            return [init_copy(yi_send.at[side], yi_recv.at[1 - side], to, 2 + side, 3 - side)]
        return [init_copy(zi_send, zi_recv.at[1 - side], to, 4 + side, 5 - side)]

    def start_faces(s, axis):
        for f in faces:
            if f[0] == axis:

                @pl.when(has[f])
                def _(f=f):
                    step_copies[axis](s, f[1], other[f]).start()

    def send(s):
        start_faces(s, 0)
        y_send[s, 0] = p_ext[s, 2 : rows_x + 2, YA : YA + 2, :]
        y_send[s, 1] = p_ext[s, 2 : rows_x + 2, YA + rows_y - 2 : YA + rows_y, :]
        start_faces(s, 1)
        z_send[s] = packed(lambda x, y: p_ext[s, 2 + x, pl.ds(YA + y, 8), :])
        start_faces(s, 2)

    def receive(s):
        for f in faces:

            @pl.when(has[f])
            def _(f=f):
                step_copies[f[0]](s, 1 - f[1], other[f]).wait_recv()

    def pressure_rows(s, x, n, last):
        at = pl.ds(x, n)
        w = vz[at]
        above_v = pltpu.roll(jnp.where(row_lane == 0, 0.0, w), depth - 1, 2)
        below_v = pltpu.roll(jnp.where(row_lane == depth - 1, 0.0, w), 1, 2)
        spread = (
            0.5 * (vx[pl.ds(x + 2, n)] - vx[at])
            + 0.5 * (vy[at, pl.ds(YA + 1, rows_y), :] - vy[at, pl.ds(YA - 1, rows_y), :])
            + (up * above_v + mid * w + low * below_v)
        )
        added = jnp.where(row_lane == 0, pltpu.roll(source[at], (depth - s) % depth, 2), 0.0)
        new = p_ext[s, pl.ds(x + 2, n), y_in, :] - 0.5 * bulk[at] * spread + added
        if last:
            p_out[at] = new
        else:
            p_ext[s + 1, pl.ds(x + 2, n), y_in, :] = new

    def velocity_x(s, at, n):
        rows = pl.ds(at, n)
        vx[rows] = vx[rows] - 0.25 * inv[rows] * (
            p_ext[s, pl.ds(at + 2, n), y_in, :] - p_ext[s, rows, y_in, :]
        )

    near_edge = (lane < 2) | (lane >= depth - 2)

    def add_packed(value, ref, x_at, y_at):
        for j in range(rows_x * halves):
            rolled = pltpu.roll(value, (-(4 * j + 2)) % depth, 1)
            at = (x_at + j // halves, pl.ds(y_at + (j % halves) * 8, 8))
            ref[at] = ref[at] + jnp.where(near_edge, rolled, 0.0)

    chunk = 4

    def inner(s, last):
        half = (rows_x - 2) // 2
        velocity_x(s, 2, half)
        velocity_x(s, 2 + half, rows_x - 2 - half)
        for i in range(0, rows_x, chunk):
            at = pl.ds(i, chunk)
            at_p = pl.ds(i + 2, chunk)
            here = p_ext[s, at_p, y_in, :]
            rho = inv[pl.ds(i + 1, chunk)]
            vy[at, y_in, :] = vy[at, y_in, :] - 0.25 * rho * (
                p_ext[s, at_p, pl.ds(YA + 1, rows_y), :] - p_ext[s, at_p, pl.ds(YA - 1, rows_y), :]
            )
            above_p = pltpu.roll(jnp.where(row_lane == 0, 0.0, here), depth - 1, 2)
            below_p = pltpu.roll(jnp.where(row_lane == depth - 1, 0.0, here), 1, 2)
            vz[at] = vz[at] - 0.5 * rho * (up * above_p + mid * here + low * below_p)
        for i in range(2, rows_x - 2, chunk):
            pressure_rows(s, i, chunk, last)

    def outer(s, last):
        velocity_x(s, 0, 2)
        velocity_x(s, rows_x, 2)
        pressure_rows(s, 0, 2, last)
        pressure_rows(s, rows_x - 2, 2, last)

        ref, x_at, y_at = (p_out, 0, 0) if last else (p_ext.at[s + 1], 2, YA)
        rows = pl.ds(x_at, rows_x)
        for side, edge, after, sign in ((0, 0, 1, 0.25), (1, rows_y - 1, rows_y - 2, -0.25)):
            near = y_recv[s, side, :, 1 - side : 2 - side, :]
            far = y_recv[s, side, :, side : side + 1, :]
            halo_v = vy_edge[side] - sign * inv_y[side] * (
                y_send[s, side, :, side : side + 1, :] - far
            )
            vy_edge[side] = halo_v
            change = sign * inv[1 : rows_x + 1, edge : edge + 1, :] * near
            at_v = (slice(None), slice(YA + edge, YA + edge + 1), slice(None))
            vy[at_v] = vy[at_v] + change
            at_edge = (rows, pl.ds(y_at + edge, 1))
            ref[at_edge] = ref[at_edge] + sign * bulk[:, edge : edge + 1, :] * halo_v
            at_after = (rows, pl.ds(y_at + after, 1))
            ref[at_after] = ref[at_after] + sign * bulk[:, after : after + 1, :] * change

        own = z_send[s]
        halo = jnp.where(quad < 2, z_recv[s, 0], z_recv[s, 1])
        above = pltpu.roll(jnp.where(quad == 2, own, halo), depth - 1, 1)
        below = pltpu.roll(jnp.where(quad == 1, own, halo), 1, 1)
        edge = vz_edge[...] - 0.5 * pack_edge[...] * (
            up_e * above + mid_e * halo + low_e * below
        )
        vz_edge[...] = edge
        change = -0.5 * zi_send[1] * jnp.where(
            quad == 1,
            up_o * pltpu.roll(halo, depth - 1, 1),
            jnp.where(quad == 2, low_o * pltpu.roll(halo, 1, 1), 0.0),
        )
        vz_change[...] = change
        ahead = pltpu.roll(jnp.where(quad == 2, edge, change), depth - 1, 1)
        behind = pltpu.roll(jnp.where(quad == 1, edge, change), 1, 1)
        spread = jnp.where(quad < 2, up_o * ahead, low_o * behind) + mid_o * change
        add_packed(-0.5 * bulk_pack[...] * spread, ref, x_at, y_at)

    count = sum(has[f].astype(jnp.int32) for f in faces)
    count = count + jnp.where(at_sea, tiles - 1 + n_z - 1, 0)
    loads[0].wait()
    pl.semaphore_wait(barrier, count)
    send(0)
    for load in loads[1:]:
        load.wait()
    zi_send[0] = packed(lambda x, y: vz[x, pl.ds(y, 8), :])
    zi_send[1] = packed(lambda x, y: inv[1 + x, pl.ds(y, 8), :])
    for side, y in ((0, 0), (1, rows_y - 1)):
        yi_send[side, :, 0:1, :] = vy[:, YA + y : YA + y + 1, :]
        yi_send[side, :, 1:2, :] = inv[1 : rows_x + 1, y : y + 1, :]
    for f in faces:

        @pl.when(has[f])
        def _(f=f):
            for copy in init_copies(*f, other[f]):
                copy.start()

    cell_x = gx_ref[...] - me[0] * rows_x
    cell_y = gy_ref[...] - me[1] * rows_y
    inside = (cell_x >= 0) & (cell_x < rows_x) & (cell_y >= 0) & (cell_y < rows_y)
    cell = jnp.where(inside, cell_x * rows_y + cell_y, -1)
    gauges = cell.shape[1]

    def three_parts(value):
        high = value.astype(jnp.bfloat16).astype(F32)
        rest = value - high
        middle = rest.astype(jnp.bfloat16).astype(F32)
        return high, middle, rest - middle

    @pl.when(me[2] != 0)
    def _():
        source[...] = jnp.zeros_like(source)

    @pl.when(me[2] == 0)
    def _():
        hot = lax.broadcasted_iota(jnp.int32, (cells, gauges), 0) == cell
        hot = hot.astype(F32).astype(jnp.bfloat16)
        scaled = jnp.concatenate(
            [0.5 * misfit_ref[...], jnp.zeros((depth - ITERS, gauges), F32)], axis=0
        )
        planes = jnp.zeros((cells, depth), F32)
        for value in three_parts(scaled):
            planes = planes + lax.dot_general(
                hot, value.astype(jnp.bfloat16), NT, preferred_element_type=F32
            )
        source[...] = planes.reshape(rows_x, rows_y, depth)

    nodes = patch_ref.shape[-1]
    patches = slot_ref.shape[1]
    per = patches // tiles
    shift = per.bit_length() - 1
    assert per == 1 << shift and per == 128
    block = min(patches, 1024)

    def slot_tables():
        patch = patch_ref[...].reshape(1, nodes)
        slot_parts = jnp.zeros((8, nodes), F32)
        first_row = lax.broadcasted_iota(jnp.int32, (8, block), 0) == 0
        for at in range(0, patches, block):
            slots = slot_ref[:, at : at + block]
            table = jnp.where(first_row, slots >> shift, slots & (per - 1)).astype(F32)
            hot = lax.broadcasted_iota(jnp.int32, (block, nodes), 0) + at == patch
            slot_parts = slot_parts + jnp.dot(
                table.astype(jnp.bfloat16),
                hot.astype(F32).astype(jnp.bfloat16),
                preferred_element_type=F32,
            )
        slot = (slot_parts[0:1] * per + slot_parts[1:2]).astype(jnp.int32)
        for at in range(0, patches, block):
            hot = lax.broadcasted_iota(jnp.int32, (block, nodes), 0) + at == slot
            slot_hot[pl.ds(at, block), :] = hot.astype(F32).astype(jnp.bfloat16)
        node = lax.broadcasted_iota(jnp.int32, (depth, nodes), 1)
        spread_hot[...] = (
            lax.broadcasted_iota(jnp.int32, (depth, nodes), 0) == 4 * (node >> 3) + 2
        ).astype(F32).astype(jnp.bfloat16)

    def slip_copy(o_x, o_y, source_tile):
        return pltpu.make_async_remote_copy(
            src_ref=part.at[o_x * n_y + o_y],
            dst_ref=got.at[source_tile],
            send_sem=slip_send.at[o_x * n_y + o_y],
            recv_sem=slip_recv.at[source_tile],
            device_id=(o_x, o_y, me[2]),
            device_id_type=MESH_ID,
        )

    def depth_copy(c, slot):
        return pltpu.make_async_remote_copy(
            src_ref=total,
            dst_ref=got_all.at[slot],
            send_sem=depth_send.at[c],
            recv_sem=depth_recv.at[slot],
            device_id=(me[0], me[1], c),
            device_id_type=MESH_ID,
        )

    my_slot = jnp.where(me[2] >= root, 1, 0)

    def finish_sea(sea):
        @pl.when(at_sea)
        def _():
            mine = 0.5 * jnp.where(me[2] == root, sea, pltpu.roll(sea, 1, 1))
            values = jnp.dot(
                jnp.concatenate(three_parts(mine), axis=0).astype(jnp.bfloat16),
                spread_hot[...],
                preferred_element_type=F32,
            )
            values = values[0:8] + values[8:16] + values[16:24]
            sub = lax.broadcasted_iota(jnp.int32, (8, nodes), 0)
            col = lax.broadcasted_iota(jnp.int32, (8, nodes), 1)
            row = jnp.sum(jnp.where((col & 7) == sub, values, 0.0), axis=0, keepdims=True)
            row = row * weight_ref[...].reshape(1, nodes)
            high, middle, lowest = three_parts(row)
            split = jnp.where(
                sub == 0, high, jnp.where(sub == 1, middle, jnp.where(sub == 2, lowest, 0.0))
            ).astype(jnp.bfloat16)
            for at in range(0, patches, block):
                sums = lax.dot_general(
                    split, slot_hot[pl.ds(at, block), :], NT, preferred_element_type=F32
                )
                sums = jnp.sum(sums, axis=0, keepdims=True)
                for o in range(block // per):
                    part[at // per + o] = sums[:, o * per : (o + 1) * per]
            got[tile] = part[tile]
            each_tile(lambda o_x, o_y: slip_copy(o_x, o_y, tile).start())

    def owner_sums():
        @pl.when(at_sea)
        def _():
            each_tile(lambda o_x, o_y: slip_copy(o_x, o_y, o_x * n_y + o_y).wait_recv())
            total[...] = jnp.sum(got[...], axis=0)
            got_all[my_slot] = total[...]
            for c in range(n_z):

                @pl.when(me[2] != c)
                def _(c=c):
                    depth_copy(c, my_slot).start()

    bulk_pack[...] = packed(lambda x, y: bulk[x, pl.ds(y, 8), :])

    def receive_start():
        for f in faces:

            @pl.when(has[f])
            def _(f=f):
                for copy in init_copies(f[0], 1 - f[1], other[f]):
                    copy.wait_recv()

        for side in (0, 1):
            vy_edge[side] = yi_recv[side, :, 0:1, :]
            inv_y[side] = yi_recv[side, :, 1:2, :]
        kept = (quad == 1) | (quad == 2)
        vz_edge[...] = jnp.where(
            kept, jnp.where(quad == 1, zi_recv[0, 0], zi_recv[1, 0]), 0.0
        )
        pack_edge[...] = jnp.where(
            kept, jnp.where(quad == 1, zi_recv[0, 1], zi_recv[1, 1]), 0.0
        )

    sea = z_send[0]
    for s in range(ITERS):
        last = s == ITERS - 1
        if s > 0:
            send(s)
            sea = sea + z_send[s]
            if last:
                finish_sea(sea)
            add_packed(vz_change[...], vz, 0, 0)
        inner(s, last)
        if s == 1:
            pl.when(at_sea)(slot_tables)
        receive(s)
        if s == 0:
            receive_start()
        if last:
            owner_sums()
        outer(s, last)
    add_packed(vz_change[...], vz, 0, 0)
    v_out[0] = vx[1 : rows_x + 1]
    v_out[1] = vy[:, YA : YA + rows_y, :]
    v_out[2] = vz[...]

    for slot_at, c in ((0, root - 1), (1, root)):

        @pl.when(me[2] != c)
        def _(slot_at=slot_at):
            depth_copy(0, slot_at).wait_recv()

    sums = got_all[0] + got_all[1]
    piece = per // n_z
    picked = sums[:, 0:piece]
    for c in range(1, n_z):
        picked = jnp.where(me[2] == c, sums[:, c * piece : (c + 1) * piece], picked)
    slip_out[...] = picked

    for f in faces:

        @pl.when(has[f])
        def _(f=f):
            for copy in init_copies(*f, other[f]):
                copy.wait_send()
            for s in range(ITERS):
                step_copies[f[0]](s, f[1], other[f]).wait_send()

    @pl.when(at_sea)
    def _():
        each_tile(lambda o_x, o_y: slip_copy(o_x, o_y, tile).wait_send())
        for c in range(n_z):

            @pl.when(me[2] != c)
            def _(c=c):
                depth_copy(c, my_slot).wait_send()


def write_out(p_in, v_in, slip_in, p_out, v_out, slip_out, sem):
    copies = [
        pltpu.make_async_copy(src, dst, sem.at[n])
        for n, (src, dst) in enumerate([(v_in, v_out), (p_in, p_out), (slip_in, slip_out)])
    ]
    for copy in copies:
        copy.start()
    for copy in copies:
        copy.wait()


def local(sizes, pressure, velocity, inv_density, bulk, node_weight, node_patch, patch_slot,
          gauge_x, gauge_y, gauge_misfit):
    rows_x, rows_y, depth = pressure.shape
    n_x, n_y, n_z = sizes
    tiles = n_x * n_y
    nodes = node_patch.shape[-1]
    patches = patch_slot.shape[0]
    per = patches // tiles
    wide_y = rows_y + 2 * YA
    box = (rows_x, rows_y, depth)
    vmem = pl.BlockSpec(memory_space=pltpu.VMEM)
    hbm = pl.BlockSpec(memory_space=pltpu.HBM)
    gauges = gauge_x.shape[0]
    scratch = [
        pltpu.VMEM((1, 1, nodes), F32),
        pltpu.VMEM((1, 1, nodes), jnp.int32),
        pltpu.VMEM((1, patches), jnp.int32),
        pltpu.VMEM((1, gauges), jnp.int32),
        pltpu.VMEM((1, gauges), jnp.int32),
        pltpu.VMEM((ITERS, gauges), F32),
        pltpu.VMEM((ITERS, rows_x + 4, wide_y, depth), F32),
        pltpu.VMEM((rows_x + 2, rows_y, depth), F32),
        pltpu.VMEM((rows_x, wide_y, depth), F32),
        pltpu.VMEM(box, F32),
        pltpu.VMEM((rows_x + 2, rows_y, depth), F32),
        pltpu.VMEM((2, rows_x, 1, depth), F32),
        pltpu.VMEM(box, F32),
        pltpu.VMEM((8, depth), F32),
        pltpu.VMEM((8, depth), F32),
        pltpu.VMEM((2, rows_x, 1, depth), F32),
        pltpu.VMEM((8, depth), F32),
        pltpu.VMEM((8, depth), F32),
        pltpu.VMEM((ITERS, 2, rows_x, 2, depth), F32),
        pltpu.VMEM((ITERS, 2, rows_x, 2, depth), F32),
        pltpu.VMEM((ITERS, 8, depth), F32),
        pltpu.VMEM((ITERS, 2, 8, depth), F32),
        pltpu.VMEM((2, rows_x, 2, depth), F32),
        pltpu.VMEM((2, rows_x, 2, depth), F32),
        pltpu.VMEM((2, 8, depth), F32),
        pltpu.VMEM((2, 2, 8, depth), F32),
        pltpu.VMEM(box, F32),
        pltpu.VMEM((patches, nodes), jnp.bfloat16),
        pltpu.VMEM((depth, nodes), jnp.bfloat16),
        pltpu.VMEM((tiles, 1, per), F32),
        pltpu.VMEM((tiles, 1, per), F32),
        pltpu.VMEM((1, per), F32),
        pltpu.VMEM((2, 1, per), F32),
        pltpu.SemaphoreType.DMA((12,)),
        pltpu.SemaphoreType.DMA((ITERS, 6)),
        pltpu.SemaphoreType.DMA((ITERS, 6)),
        pltpu.SemaphoreType.DMA((8,)),
        pltpu.SemaphoreType.DMA((8,)),
        pltpu.SemaphoreType.DMA((tiles,)),
        pltpu.SemaphoreType.DMA((tiles,)),
        pltpu.SemaphoreType.DMA((n_z,)),
        pltpu.SemaphoreType.DMA((2,)),
    ]
    colored = [pltpu.VMEM(box, F32), pltpu.VMEM((3,) + box, F32), pltpu.VMEM((1, per // n_z), F32)]
    shapes = [
        jax.ShapeDtypeStruct(box, F32),
        jax.ShapeDtypeStruct((3,) + box, F32),
        jax.ShapeDtypeStruct((1, per // n_z), F32),
    ]
    p_new, v_new, slip = pl.pallas_call(
        functools.partial(kernel, sizes),
        out_shape=colored,
        in_specs=[hbm] * 10,
        out_specs=[vmem] * 3,
        scratch_shapes=scratch,
        compiler_params=pltpu.CompilerParams(
            collective_id=0, has_side_effects=True, vmem_limit_bytes=64 * 1024 * 1024 - 1400 * 1024
        ),
    )(
        pressure,
        velocity,
        inv_density,
        bulk,
        node_weight,
        node_patch,
        patch_slot.reshape(1, patches),
        gauge_x.reshape(1, -1),
        gauge_y.reshape(1, -1),
        gauge_misfit,
    )
    anywhere = pl.BlockSpec(memory_space=pl.ANY)
    p_new, v_new, slip = pl.pallas_call(
        write_out,
        out_shape=shapes,
        in_specs=[anywhere] * 3,
        out_specs=[anywhere] * 3,
        scratch_shapes=[pltpu.SemaphoreType.DMA((3,))],
        compiler_params=pltpu.CompilerParams(vmem_limit_bytes=2 * 1024 * 1024),
    )(p_new, v_new, slip)
    return p_new, v_new, slip.reshape(per // n_z)


def solution(mesh):
    placed = (
        P("gx", "gy", "gz"),
        P(None, "gx", "gy", "gz"),
        P("gx", "gy", "gz"),
        P("gx", "gy", "gz"),
        P("gx", "gy", None),
        P("gx", "gy", None),
        P(),
        P(),
        P(),
        P(),
    )
    sizes = tuple(mesh.shape[a] for a in AXES)
    return jax.shard_map(
        functools.partial(local, sizes),
        mesh=mesh,
        in_specs=placed,
        out_specs=(P("gx", "gy", "gz"), P(None, "gx", "gy", "gz"), P(("gx", "gy", "gz"))),
        check_vma=False,
    )
```

```python
import functools

import jax
import jax.numpy as jnp
from jax import lax
from jax.experimental import pallas as pl
from jax.experimental.pallas import tpu as pltpu
from jax.sharding import PartitionSpec as P

ITERS = 4
MESH_ID = pl.DeviceIdType.MESH
AXES = ("gx", "gy", "gz")
YA = 8
F32 = jnp.float32
NT = (((1,), (1,)), ((), ()))


def kernel(
    sizes,
    p_in,
    v_in,
    d_in,
    b_in,
    weight_in,
    patch_in,
    slot_in,
    gx_in,
    gy_in,
    misfit_in,
    p_out,
    v_out,
    slip_out,
    weight_ref,
    patch_ref,
    slot_ref,
    gx_ref,
    gy_ref,
    misfit_ref,
    p_ext,
    vx,
    vy,
    vz,
    inv,
    inv_y,
    bulk,
    pack_edge,
    vz_edge,
    vy_edge,
    vz_change,
    bulk_pack,
    y_send,
    y_recv,
    z_send,
    z_recv,
    yi_send,
    yi_recv,
    zi_send,
    zi_recv,
    source,
    slot_hot,
    spread_hot,
    part,
    got,
    total,
    got_all,
    load_sem,
    send_sem,
    recv_sem,
    init_send,
    init_recv,
    slip_send,
    slip_recv,
    depth_send,
    depth_recv,
):
    n_x, n_y, n_z = sizes
    rows_x, rows_y, depth = p_in.shape
    cells = rows_x * rows_y
    halves = rows_y // 8
    me = [lax.axis_index(a) for a in AXES]
    tiles = n_x * n_y
    tile = me[0] * n_y + me[1]
    root = n_z // 2
    has = {}
    other = {}
    for a in range(3):
        has[a, 0] = me[a] > 0
        has[a, 1] = me[a] < sizes[a] - 1
        for side in (0, 1):
            to = list(me)
            to[a] = me[a] + (2 * side - 1)
            other[a, side] = tuple(to)
    faces = [(a, side) for a in range(3) for side in (0, 1) if sizes[a] > 1]

    y_in = pl.ds(YA, rows_y)
    x_in = pl.ds(2, rows_x)
    loads = [
        pltpu.make_async_copy(p_in, p_ext.at[0, x_in, y_in], load_sem.at[0]),
        pltpu.make_async_copy(d_in, inv.at[pl.ds(1, rows_x)], load_sem.at[1]),
        pltpu.make_async_copy(v_in.at[2], vz, load_sem.at[2]),
        pltpu.make_async_copy(v_in.at[1], vy.at[:, y_in], load_sem.at[3]),
        pltpu.make_async_copy(v_in.at[0], vx.at[pl.ds(1, rows_x)], load_sem.at[4]),
        pltpu.make_async_copy(b_in, bulk, load_sem.at[5]),
        pltpu.make_async_copy(weight_in, weight_ref, load_sem.at[6]),
        pltpu.make_async_copy(patch_in, patch_ref, load_sem.at[7]),
        pltpu.make_async_copy(slot_in, slot_ref, load_sem.at[8]),
        pltpu.make_async_copy(gx_in, gx_ref, load_sem.at[9]),
        pltpu.make_async_copy(gy_in, gy_ref, load_sem.at[10]),
        pltpu.make_async_copy(misfit_in, misfit_ref, load_sem.at[11]),
    ]
    for load in loads:
        load.start()

    barrier = pltpu.get_barrier_semaphore()
    for f in faces:

        @pl.when(has[f])
        def _(f=f):
            pl.semaphore_signal(barrier, inc=1, device_id=other[f], device_id_type=MESH_ID)

    at_sea = (me[2] == root) | (me[2] == root - 1)

    def each_tile(act):
        def one(o_x, o_y):
            @pl.when((o_x != me[0]) | (o_y != me[1]))
            def _():
                act(o_x, o_y)

        if tiles <= 8:
            for o in range(tiles):
                one(o // n_y, o % n_y)
        else:

            def row(o_x, _):
                def column(o_y, _):
                    one(o_x, o_y)
                    return 0

                return lax.fori_loop(0, n_y, column, 0)

            lax.fori_loop(0, n_x, row, 0)

    def greet(o_x, o_y):
        pl.semaphore_signal(
            barrier, inc=1, device_id=(o_x, o_y, me[2]), device_id_type=MESH_ID
        )

    @pl.when(at_sea)
    def _():
        each_tile(greet)

    for c in (root - 1, root):

        @pl.when(me[2] != c)
        def _(c=c):
            pl.semaphore_signal(
                barrier, inc=1, device_id=(me[0], me[1], c), device_id_type=MESH_ID
            )

    for y in (YA - 1, YA + rows_y):
        zero = jnp.zeros((rows_x, 1, depth), F32)
        vy[:, y : y + 1, :] = zero
        for s in range(ITERS):
            p_ext[s, 2 : rows_x + 2, y : y + 1, :] = zero

    for side in (0, 1):

        @pl.when(jnp.logical_not(has[0, side]))
        def _(side=side):
            at = 0 if side == 0 else rows_x + 2
            p_ext[:, pl.ds(at, 2), :, :] = jnp.zeros_like(p_ext[:, pl.ds(at, 2), :, :])
            one = 0 if side == 0 else rows_x + 1
            vx[one] = jnp.zeros_like(vx[one])
            inv[one] = jnp.zeros_like(inv[one])

        @pl.when(jnp.logical_not(has[1, side]))
        def _(side=side):
            y_recv[:, side] = jnp.zeros_like(y_recv[:, side])
            yi_recv[side] = jnp.zeros_like(yi_recv[side])

        @pl.when(jnp.logical_not(has[2, side]))
        def _(side=side):
            z_recv[:, side] = jnp.zeros_like(z_recv[:, side])
            zi_recv[side] = jnp.zeros_like(zi_recv[side])

    lane = lax.broadcasted_iota(jnp.int32, (8, depth), 1)
    quad = lane & 3
    group = lane >> 2

    def packed(read):
        q = jnp.zeros((8, depth), F32)
        for j in range(rows_x * halves):
            rolled = pltpu.roll(read(j // halves, (j % halves) * 8), (4 * j + 2) % depth, 1)
            q = jnp.where(group == j, rolled, q)
        return q

    def coefs(level):
        first = root * depth
        last_ocean = level == first - 1
        crust = level == first
        up = jnp.where(crust, 1.0, 0.5).astype(F32)
        mid = jnp.where(last_ocean, 0.5, jnp.where(crust, -1.5, 0.0)).astype(F32)
        low = jnp.where(last_ocean, -1.0, jnp.where(crust, 0.5, -0.5)).astype(F32)
        return up, mid, low

    row_lane = lax.broadcasted_iota(jnp.int32, (1, 1, depth), 2)
    up, mid, low = coefs(me[2] * depth + row_lane)
    up_e, mid_e, low_e = coefs(
        jnp.where(quad == 1, me[2] * depth - 1, (me[2] + 1) * depth)
    )

    up_o, mid_o, low_o = coefs(
        me[2] * depth + jnp.where(quad < 2, depth - 2 + quad, quad - 2)
    )

    def copy_x(s, side, to):
        src, dst = (2, rows_x + 2) if side == 0 else (rows_x, 0)
        return pltpu.make_async_remote_copy(
            src_ref=p_ext.at[s, pl.ds(src, 2), y_in],
            dst_ref=p_ext.at[s, pl.ds(dst, 2), y_in],
            send_sem=send_sem.at[s, side],
            recv_sem=recv_sem.at[s, 1 - side],
            device_id=to,
            device_id_type=MESH_ID,
        )

    def copy_y(s, side, to):
        return pltpu.make_async_remote_copy(
            src_ref=y_send.at[s, side],
            dst_ref=y_recv.at[s, 1 - side],
            send_sem=send_sem.at[s, 2 + side],
            recv_sem=recv_sem.at[s, 3 - side],
            device_id=to,
            device_id_type=MESH_ID,
        )

    def copy_z(s, side, to):
        return pltpu.make_async_remote_copy(
            src_ref=z_send.at[s],
            dst_ref=z_recv.at[s, 1 - side],
            send_sem=send_sem.at[s, 4 + side],
            recv_sem=recv_sem.at[s, 5 - side],
            device_id=to,
            device_id_type=MESH_ID,
        )

    step_copies = {0: copy_x, 1: copy_y, 2: copy_z}

    def init_copy(src, dst, to, n, back):
        return pltpu.make_async_remote_copy(
            src_ref=src,
            dst_ref=dst,
            send_sem=init_send.at[n],
            recv_sem=init_recv.at[back],
            device_id=to,
            device_id_type=MESH_ID,
        )

    def init_copies(a, side, to):
        if a == 0:
            src, dst = (0, rows_x + 1) if side == 0 else (rows_x - 1, 0)
            return [
                init_copy(
                    v_in.at[0, pl.ds(src, 1)], vx.at[pl.ds(dst, 1)], to, side, 1 - side
                ),
                init_copy(
                    inv.at[pl.ds(src + 1, 1)], inv.at[pl.ds(dst, 1)], to, 6 + side, 7 - side
                ),
            ]
        if a == 1:
            return [init_copy(yi_send.at[side], yi_recv.at[1 - side], to, 2 + side, 3 - side)]
        return [init_copy(zi_send, zi_recv.at[1 - side], to, 4 + side, 5 - side)]

    def start_faces(s, axis):
        for f in faces:
            if f[0] == axis:

                @pl.when(has[f])
                def _(f=f):
                    step_copies[axis](s, f[1], other[f]).start()

    def send(s):
        start_faces(s, 0)
        y_send[s, 0] = p_ext[s, 2 : rows_x + 2, YA : YA + 2, :]
        y_send[s, 1] = p_ext[s, 2 : rows_x + 2, YA + rows_y - 2 : YA + rows_y, :]
        start_faces(s, 1)
        z_send[s] = packed(lambda x, y: p_ext[s, 2 + x, pl.ds(YA + y, 8), :])
        start_faces(s, 2)

    def receive(s):
        for f in faces:

            @pl.when(has[f])
            def _(f=f):
                step_copies[f[0]](s, 1 - f[1], other[f]).wait_recv()

    def pressure_rows(s, x, n):
        at = pl.ds(x, n)
        w = vz[at]
        above_v = pltpu.roll(jnp.where(row_lane == 0, 0.0, w), depth - 1, 2)
        below_v = pltpu.roll(jnp.where(row_lane == depth - 1, 0.0, w), 1, 2)
        spread = (
            0.5 * (vx[pl.ds(x + 2, n)] - vx[at])
            + 0.5 * (vy[at, pl.ds(YA + 1, rows_y), :] - vy[at, pl.ds(YA - 1, rows_y), :])
            + (up * above_v + mid * w + low * below_v)
        )
        added = jnp.where(row_lane == 0, pltpu.roll(source[at], (depth - s) % depth, 2), 0.0)
        new = p_ext[s, pl.ds(x + 2, n), y_in, :] - 0.5 * bulk[at] * spread + added
        p_ext[s + 1, pl.ds(x + 2, n), y_in, :] = new

    def velocity_x(s, at, n):
        rows = pl.ds(at, n)
        vx[rows] = vx[rows] - 0.25 * inv[rows] * (
            p_ext[s, pl.ds(at + 2, n), y_in, :] - p_ext[s, rows, y_in, :]
        )

    near_edge = (lane < 2) | (lane >= depth - 2)

    def add_packed(value, ref, x_at, y_at):
        for j in range(rows_x * halves):
            rolled = pltpu.roll(value, (-(4 * j + 2)) % depth, 1)
            at = (x_at + j // halves, pl.ds(y_at + (j % halves) * 8, 8))
            ref[at] = ref[at] + jnp.where(near_edge, rolled, 0.0)

    chunk = 4

    def inner(s):
        half = (rows_x - 2) // 2
        velocity_x(s, 2, half)
        velocity_x(s, 2 + half, rows_x - 2 - half)
        for i in range(0, rows_x, chunk):
            at = pl.ds(i, chunk)
            at_p = pl.ds(i + 2, chunk)
            here = p_ext[s, at_p, y_in, :]
            rho = inv[pl.ds(i + 1, chunk)]
            vy[at, y_in, :] = vy[at, y_in, :] - 0.25 * rho * (
                p_ext[s, at_p, pl.ds(YA + 1, rows_y), :] - p_ext[s, at_p, pl.ds(YA - 1, rows_y), :]
            )
            above_p = pltpu.roll(jnp.where(row_lane == 0, 0.0, here), depth - 1, 2)
            below_p = pltpu.roll(jnp.where(row_lane == depth - 1, 0.0, here), 1, 2)
            vz[at] = vz[at] - 0.5 * rho * (up * above_p + mid * here + low * below_p)
        for i in range(2, rows_x - 2, chunk):
            pressure_rows(s, i, chunk)

    def outer(s):
        velocity_x(s, 0, 2)
        velocity_x(s, rows_x, 2)
        pressure_rows(s, 0, 2)
        pressure_rows(s, rows_x - 2, 2)

        ref, x_at, y_at = p_ext.at[s + 1], 2, YA
        rows = pl.ds(x_at, rows_x)
        for side, edge, after, sign in ((0, 0, 1, 0.25), (1, rows_y - 1, rows_y - 2, -0.25)):
            near = y_recv[s, side, :, 1 - side : 2 - side, :]
            far = y_recv[s, side, :, side : side + 1, :]
            halo_v = vy_edge[side] - sign * inv_y[side] * (
                y_send[s, side, :, side : side + 1, :] - far
            )
            vy_edge[side] = halo_v
            change = sign * inv[1 : rows_x + 1, edge : edge + 1, :] * near
            at_v = (slice(None), slice(YA + edge, YA + edge + 1), slice(None))
            vy[at_v] = vy[at_v] + change
            at_edge = (rows, pl.ds(y_at + edge, 1))
            ref[at_edge] = ref[at_edge] + sign * bulk[:, edge : edge + 1, :] * halo_v
            at_after = (rows, pl.ds(y_at + after, 1))
            ref[at_after] = ref[at_after] + sign * bulk[:, after : after + 1, :] * change

        own = z_send[s]
        halo = jnp.where(quad < 2, z_recv[s, 0], z_recv[s, 1])
        above = pltpu.roll(jnp.where(quad == 2, own, halo), depth - 1, 1)
        below = pltpu.roll(jnp.where(quad == 1, own, halo), 1, 1)
        edge = vz_edge[...] - 0.5 * pack_edge[...] * (
            up_e * above + mid_e * halo + low_e * below
        )
        vz_edge[...] = edge
        change = -0.5 * zi_send[1] * jnp.where(
            quad == 1,
            up_o * pltpu.roll(halo, depth - 1, 1),
            jnp.where(quad == 2, low_o * pltpu.roll(halo, 1, 1), 0.0),
        )
        vz_change[...] = change
        ahead = pltpu.roll(jnp.where(quad == 2, edge, change), depth - 1, 1)
        behind = pltpu.roll(jnp.where(quad == 1, edge, change), 1, 1)
        spread = jnp.where(quad < 2, up_o * ahead, low_o * behind) + mid_o * change
        add_packed(-0.5 * bulk_pack[...] * spread, ref, x_at, y_at)

    count = sum(has[f].astype(jnp.int32) for f in faces)
    count = count + jnp.where(at_sea, tiles - 1 + n_z - 1, 0)
    loads[0].wait()
    pl.semaphore_wait(barrier, count)
    send(0)
    for load in loads[1:]:
        load.wait()
    zi_send[0] = packed(lambda x, y: vz[x, pl.ds(y, 8), :])
    zi_send[1] = packed(lambda x, y: inv[1 + x, pl.ds(y, 8), :])
    for side, y in ((0, 0), (1, rows_y - 1)):
        yi_send[side, :, 0:1, :] = vy[:, YA + y : YA + y + 1, :]
        yi_send[side, :, 1:2, :] = inv[1 : rows_x + 1, y : y + 1, :]
    for f in faces:

        @pl.when(has[f])
        def _(f=f):
            for copy in init_copies(*f, other[f]):
                copy.start()

    cell_x = gx_ref[...] - me[0] * rows_x
    cell_y = gy_ref[...] - me[1] * rows_y
    inside = (cell_x >= 0) & (cell_x < rows_x) & (cell_y >= 0) & (cell_y < rows_y)
    cell = jnp.where(inside, cell_x * rows_y + cell_y, -1)
    gauges = cell.shape[1]

    def three_parts(value):
        high = value.astype(jnp.bfloat16).astype(F32)
        rest = value - high
        middle = rest.astype(jnp.bfloat16).astype(F32)
        return high, middle, rest - middle

    @pl.when(me[2] != 0)
    def _():
        source[...] = jnp.zeros_like(source)

    @pl.when(me[2] == 0)
    def _():
        hot = lax.broadcasted_iota(jnp.int32, (cells, gauges), 0) == cell
        hot = hot.astype(F32).astype(jnp.bfloat16)
        scaled = jnp.concatenate(
            [0.5 * misfit_ref[...], jnp.zeros((depth - ITERS, gauges), F32)], axis=0
        )
        planes = jnp.zeros((cells, depth), F32)
        for value in three_parts(scaled):
            planes = planes + lax.dot_general(
                hot, value.astype(jnp.bfloat16), NT, preferred_element_type=F32
            )
        source[...] = planes.reshape(rows_x, rows_y, depth)

    nodes = patch_ref.shape[-1]
    patches = slot_ref.shape[1]
    per = patches // tiles
    shift = per.bit_length() - 1
    assert per == 1 << shift and per == 128
    block = min(patches, 1024)

    def slot_tables():
        patch = patch_ref[...].reshape(1, nodes)
        slot_parts = jnp.zeros((8, nodes), F32)
        first_row = lax.broadcasted_iota(jnp.int32, (8, block), 0) == 0
        for at in range(0, patches, block):
            slots = slot_ref[:, at : at + block]
            table = jnp.where(first_row, slots >> shift, slots & (per - 1)).astype(F32)
            hot = lax.broadcasted_iota(jnp.int32, (block, nodes), 0) + at == patch
            slot_parts = slot_parts + jnp.dot(
                table.astype(jnp.bfloat16),
                hot.astype(F32).astype(jnp.bfloat16),
                preferred_element_type=F32,
            )
        slot = (slot_parts[0:1] * per + slot_parts[1:2]).astype(jnp.int32)
        for at in range(0, patches, block):
            hot = lax.broadcasted_iota(jnp.int32, (block, nodes), 0) + at == slot
            slot_hot[pl.ds(at, block), :] = hot.astype(F32).astype(jnp.bfloat16)
        node = lax.broadcasted_iota(jnp.int32, (depth, nodes), 1)
        spread_hot[...] = (
            lax.broadcasted_iota(jnp.int32, (depth, nodes), 0) == 4 * (node >> 3) + 2
        ).astype(F32).astype(jnp.bfloat16)

    def slip_copy(o_x, o_y, source_tile):
        return pltpu.make_async_remote_copy(
            src_ref=part.at[o_x * n_y + o_y],
            dst_ref=got.at[source_tile],
            send_sem=slip_send.at[o_x * n_y + o_y],
            recv_sem=slip_recv.at[source_tile],
            device_id=(o_x, o_y, me[2]),
            device_id_type=MESH_ID,
        )

    def depth_copy(c, slot):
        return pltpu.make_async_remote_copy(
            src_ref=total,
            dst_ref=got_all.at[slot],
            send_sem=depth_send.at[c],
            recv_sem=depth_recv.at[slot],
            device_id=(me[0], me[1], c),
            device_id_type=MESH_ID,
        )

    my_slot = jnp.where(me[2] >= root, 1, 0)

    def finish_sea(sea):
        @pl.when(at_sea)
        def _():
            mine = 0.5 * jnp.where(me[2] == root, sea, pltpu.roll(sea, 1, 1))
            values = jnp.dot(
                jnp.concatenate(three_parts(mine), axis=0).astype(jnp.bfloat16),
                spread_hot[...],
                preferred_element_type=F32,
            )
            values = values[0:8] + values[8:16] + values[16:24]
            sub = lax.broadcasted_iota(jnp.int32, (8, nodes), 0)
            col = lax.broadcasted_iota(jnp.int32, (8, nodes), 1)
            row = jnp.sum(jnp.where((col & 7) == sub, values, 0.0), axis=0, keepdims=True)
            row = row * weight_ref[...].reshape(1, nodes)
            high, middle, lowest = three_parts(row)
            split = jnp.where(
                sub == 0, high, jnp.where(sub == 1, middle, jnp.where(sub == 2, lowest, 0.0))
            ).astype(jnp.bfloat16)
            for at in range(0, patches, block):
                sums = lax.dot_general(
                    split, slot_hot[pl.ds(at, block), :], NT, preferred_element_type=F32
                )
                sums = jnp.sum(sums, axis=0, keepdims=True)
                for o in range(block // per):
                    part[at // per + o] = sums[:, o * per : (o + 1) * per]
            got[tile] = part[tile]
            each_tile(lambda o_x, o_y: slip_copy(o_x, o_y, tile).start())

    def owner_sums():
        @pl.when(at_sea)
        def _():
            each_tile(lambda o_x, o_y: slip_copy(o_x, o_y, o_x * n_y + o_y).wait_recv())
            total[...] = jnp.sum(got[...], axis=0)
            got_all[my_slot] = total[...]
            for c in range(n_z):

                @pl.when(me[2] != c)
                def _(c=c):
                    depth_copy(c, my_slot).start()

    bulk_pack[...] = packed(lambda x, y: bulk[x, pl.ds(y, 8), :])

    def receive_start():
        for f in faces:

            @pl.when(has[f])
            def _(f=f):
                for copy in init_copies(f[0], 1 - f[1], other[f]):
                    copy.wait_recv()

        for side in (0, 1):
            vy_edge[side] = yi_recv[side, :, 0:1, :]
            inv_y[side] = yi_recv[side, :, 1:2, :]
        kept = (quad == 1) | (quad == 2)
        vz_edge[...] = jnp.where(
            kept, jnp.where(quad == 1, zi_recv[0, 0], zi_recv[1, 0]), 0.0
        )
        pack_edge[...] = jnp.where(
            kept, jnp.where(quad == 1, zi_recv[0, 1], zi_recv[1, 1]), 0.0
        )

    vz_change[...] = jnp.zeros_like(vz_change)

    def step(s, sea):
        @pl.when(s > 0)
        def _():
            send(s)

        sea = sea + z_send[s]
        last = s == ITERS - 1

        @pl.when(last)
        def _():
            finish_sea(sea)

        add_packed(vz_change[...], vz, 0, 0)
        inner(s)
        pl.when(at_sea & (s == 1))(slot_tables)
        receive(s)
        pl.when(s == 0)(receive_start)
        pl.when(last)(owner_sums)
        outer(s)
        return sea

    lax.fori_loop(0, ITERS, step, jnp.zeros((8, depth), F32))
    p_out[...] = p_ext[ITERS, 2 : rows_x + 2, YA : YA + rows_y, :]
    add_packed(vz_change[...], vz, 0, 0)
    v_out[0] = vx[1 : rows_x + 1]
    v_out[1] = vy[:, YA : YA + rows_y, :]
    v_out[2] = vz[...]

    for slot_at, c in ((0, root - 1), (1, root)):

        @pl.when(me[2] != c)
        def _(slot_at=slot_at):
            depth_copy(0, slot_at).wait_recv()

    sums = got_all[0] + got_all[1]
    piece = per // n_z
    picked = sums[:, 0:piece]
    for c in range(1, n_z):
        picked = jnp.where(me[2] == c, sums[:, c * piece : (c + 1) * piece], picked)
    slip_out[...] = picked

    for f in faces:

        @pl.when(has[f])
        def _(f=f):
            for copy in init_copies(*f, other[f]):
                copy.wait_send()
            for s in range(ITERS):
                step_copies[f[0]](s, f[1], other[f]).wait_send()

    @pl.when(at_sea)
    def _():
        each_tile(lambda o_x, o_y: slip_copy(o_x, o_y, tile).wait_send())
        for c in range(n_z):

            @pl.when(me[2] != c)
            def _(c=c):
                depth_copy(c, my_slot).wait_send()


def write_out(p_in, v_in, slip_in, p_out, v_out, slip_out, sem):
    copies = [
        pltpu.make_async_copy(src, dst, sem.at[n])
        for n, (src, dst) in enumerate([(v_in, v_out), (p_in, p_out), (slip_in, slip_out)])
    ]
    for copy in copies:
        copy.start()
    for copy in copies:
        copy.wait()


def local(sizes, pressure, velocity, inv_density, bulk, node_weight, node_patch, patch_slot,
          gauge_x, gauge_y, gauge_misfit):
    rows_x, rows_y, depth = pressure.shape
    n_x, n_y, n_z = sizes
    tiles = n_x * n_y
    nodes = node_patch.shape[-1]
    patches = patch_slot.shape[0]
    per = patches // tiles
    wide_y = rows_y + 2 * YA
    box = (rows_x, rows_y, depth)
    vmem = pl.BlockSpec(memory_space=pltpu.VMEM)
    hbm = pl.BlockSpec(memory_space=pltpu.HBM)
    gauges = gauge_x.shape[0]
    scratch = [
        pltpu.VMEM((1, 1, nodes), F32),
        pltpu.VMEM((1, 1, nodes), jnp.int32),
        pltpu.VMEM((1, patches), jnp.int32),
        pltpu.VMEM((1, gauges), jnp.int32),
        pltpu.VMEM((1, gauges), jnp.int32),
        pltpu.VMEM((ITERS, gauges), F32),
        pltpu.VMEM((ITERS + 1, rows_x + 4, wide_y, depth), F32),
        pltpu.VMEM((rows_x + 2, rows_y, depth), F32),
        pltpu.VMEM((rows_x, wide_y, depth), F32),
        pltpu.VMEM(box, F32),
        pltpu.VMEM((rows_x + 2, rows_y, depth), F32),
        pltpu.VMEM((2, rows_x, 1, depth), F32),
        pltpu.VMEM(box, F32),
        pltpu.VMEM((8, depth), F32),
        pltpu.VMEM((8, depth), F32),
        pltpu.VMEM((2, rows_x, 1, depth), F32),
        pltpu.VMEM((8, depth), F32),
        pltpu.VMEM((8, depth), F32),
        pltpu.VMEM((ITERS, 2, rows_x, 2, depth), F32),
        pltpu.VMEM((ITERS, 2, rows_x, 2, depth), F32),
        pltpu.VMEM((ITERS, 8, depth), F32),
        pltpu.VMEM((ITERS, 2, 8, depth), F32),
        pltpu.VMEM((2, rows_x, 2, depth), F32),
        pltpu.VMEM((2, rows_x, 2, depth), F32),
        pltpu.VMEM((2, 8, depth), F32),
        pltpu.VMEM((2, 2, 8, depth), F32),
        pltpu.VMEM(box, F32),
        pltpu.VMEM((patches, nodes), jnp.bfloat16),
        pltpu.VMEM((depth, nodes), jnp.bfloat16),
        pltpu.VMEM((tiles, 1, per), F32),
        pltpu.VMEM((tiles, 1, per), F32),
        pltpu.VMEM((1, per), F32),
        pltpu.VMEM((2, 1, per), F32),
        pltpu.SemaphoreType.DMA((12,)),
        pltpu.SemaphoreType.DMA((ITERS, 6)),
        pltpu.SemaphoreType.DMA((ITERS, 6)),
        pltpu.SemaphoreType.DMA((8,)),
        pltpu.SemaphoreType.DMA((8,)),
        pltpu.SemaphoreType.DMA((tiles,)),
        pltpu.SemaphoreType.DMA((tiles,)),
        pltpu.SemaphoreType.DMA((n_z,)),
        pltpu.SemaphoreType.DMA((2,)),
    ]
    colored = [pltpu.VMEM(box, F32), pltpu.VMEM((3,) + box, F32), pltpu.VMEM((1, per // n_z), F32)]
    shapes = [
        jax.ShapeDtypeStruct(box, F32),
        jax.ShapeDtypeStruct((3,) + box, F32),
        jax.ShapeDtypeStruct((1, per // n_z), F32),
    ]
    p_new, v_new, slip = pl.pallas_call(
        functools.partial(kernel, sizes),
        out_shape=colored,
        in_specs=[hbm] * 10,
        out_specs=[vmem] * 3,
        scratch_shapes=scratch,
        compiler_params=pltpu.CompilerParams(
            collective_id=0, has_side_effects=True, vmem_limit_bytes=64 * 1024 * 1024 - 1400 * 1024
        ),
    )(
        pressure,
        velocity,
        inv_density,
        bulk,
        node_weight,
        node_patch,
        patch_slot.reshape(1, patches),
        gauge_x.reshape(1, -1),
        gauge_y.reshape(1, -1),
        gauge_misfit,
    )
    anywhere = pl.BlockSpec(memory_space=pl.ANY)
    p_new, v_new, slip = pl.pallas_call(
        write_out,
        out_shape=shapes,
        in_specs=[anywhere] * 3,
        out_specs=[anywhere] * 3,
        scratch_shapes=[pltpu.SemaphoreType.DMA((3,))],
        compiler_params=pltpu.CompilerParams(vmem_limit_bytes=2 * 1024 * 1024),
    )(p_new, v_new, slip)
    return p_new, v_new, slip.reshape(per // n_z)


def solution(mesh):
    placed = (
        P("gx", "gy", "gz"),
        P(None, "gx", "gy", "gz"),
        P("gx", "gy", "gz"),
        P("gx", "gy", "gz"),
        P("gx", "gy", None),
        P("gx", "gy", None),
        P(),
        P(),
        P(),
        P(),
    )
    sizes = tuple(mesh.shape[a] for a in AXES)
    return jax.shard_map(
        functools.partial(local, sizes),
        mesh=mesh,
        in_specs=placed,
        out_specs=(P("gx", "gy", "gz"), P(None, "gx", "gy", "gz"), P(("gx", "gy", "gz"))),
        check_vma=False,
    )
```

```python
import functools

import jax
import jax.numpy as jnp
from jax import lax
from jax.experimental import pallas as pl
from jax.experimental.pallas import tpu as pltpu
from jax.sharding import PartitionSpec as P

ITERS = 4
MESH_ID = pl.DeviceIdType.MESH
AXES = ("gx", "gy", "gz")
YA = 8
F32 = jnp.float32
NT = (((1,), (1,)), ((), ()))


def kernel(
    sizes,
    p_in,
    v_in,
    d_in,
    b_in,
    weight_in,
    patch_in,
    slot_in,
    gx_in,
    gy_in,
    misfit_in,
    p_out,
    v_out,
    slip_out,
    weight_ref,
    patch_ref,
    slot_ref,
    gx_ref,
    gy_ref,
    misfit_ref,
    p_ext,
    vx,
    vy,
    vz,
    inv,
    inv_y,
    bulk,
    pack_edge,
    vz_edge,
    vy_edge,
    vz_change,
    bulk_pack,
    y_send,
    y_recv,
    z_send,
    z_recv,
    yi_send,
    yi_recv,
    zi_send,
    zi_recv,
    source,
    slot_hot,
    spread_hot,
    part,
    got,
    total,
    got_all,
    load_sem,
    send_sem,
    recv_sem,
    init_send,
    init_recv,
    slip_send,
    slip_recv,
    depth_send,
    depth_recv,
):
    n_x, n_y, n_z = sizes
    rows_x, rows_y, depth = p_in.shape
    cells = rows_x * rows_y
    halves = rows_y // 8
    me = [lax.axis_index(a) for a in AXES]
    tiles = n_x * n_y
    tile = me[0] * n_y + me[1]
    root = n_z // 2
    has = {}
    other = {}
    for a in range(3):
        has[a, 0] = me[a] > 0
        has[a, 1] = me[a] < sizes[a] - 1
        for side in (0, 1):
            to = list(me)
            to[a] = me[a] + (2 * side - 1)
            other[a, side] = tuple(to)
    faces = [(a, side) for a in range(3) for side in (0, 1) if sizes[a] > 1]

    y_in = pl.ds(YA, rows_y)
    x_in = pl.ds(2, rows_x)
    loads = [
        pltpu.make_async_copy(p_in, p_ext.at[0, x_in, y_in], load_sem.at[0]),
        pltpu.make_async_copy(d_in, inv.at[pl.ds(1, rows_x)], load_sem.at[1]),
        pltpu.make_async_copy(v_in.at[2], vz, load_sem.at[2]),
        pltpu.make_async_copy(v_in.at[1], vy.at[:, y_in], load_sem.at[3]),
        pltpu.make_async_copy(v_in.at[0], vx.at[pl.ds(1, rows_x)], load_sem.at[4]),
        pltpu.make_async_copy(b_in, bulk, load_sem.at[5]),
        pltpu.make_async_copy(weight_in, weight_ref, load_sem.at[6]),
        pltpu.make_async_copy(patch_in, patch_ref, load_sem.at[7]),
        pltpu.make_async_copy(slot_in, slot_ref, load_sem.at[8]),
        pltpu.make_async_copy(gx_in, gx_ref, load_sem.at[9]),
        pltpu.make_async_copy(gy_in, gy_ref, load_sem.at[10]),
        pltpu.make_async_copy(misfit_in, misfit_ref, load_sem.at[11]),
    ]
    for load in loads:
        load.start()

    barrier = pltpu.get_barrier_semaphore()
    for f in faces:

        @pl.when(has[f])
        def _(f=f):
            pl.semaphore_signal(barrier, inc=1, device_id=other[f], device_id_type=MESH_ID)

    at_sea = (me[2] == root) | (me[2] == root - 1)

    def each_tile(act):
        def one(o_x, o_y):
            @pl.when((o_x != me[0]) | (o_y != me[1]))
            def _():
                act(o_x, o_y)

        if tiles <= 8:
            for o in range(tiles):
                one(o // n_y, o % n_y)
        else:

            def row(o_x, _):
                def column(o_y, _):
                    one(o_x, o_y)
                    return 0

                return lax.fori_loop(0, n_y, column, 0)

            lax.fori_loop(0, n_x, row, 0)

    def greet(o_x, o_y):
        pl.semaphore_signal(
            barrier, inc=1, device_id=(o_x, o_y, me[2]), device_id_type=MESH_ID
        )

    @pl.when(at_sea)
    def _():
        each_tile(greet)

    for c in (root - 1, root):

        @pl.when(me[2] != c)
        def _(c=c):
            pl.semaphore_signal(
                barrier, inc=1, device_id=(me[0], me[1], c), device_id_type=MESH_ID
            )

    for y in (YA - 1, YA + rows_y):
        zero = jnp.zeros((rows_x, 1, depth), F32)
        vy[:, y : y + 1, :] = zero
        for s in range(ITERS):
            p_ext[s, 2 : rows_x + 2, y : y + 1, :] = zero

    for side in (0, 1):

        @pl.when(jnp.logical_not(has[0, side]))
        def _(side=side):
            at = 0 if side == 0 else rows_x + 2
            p_ext[:, pl.ds(at, 2), :, :] = jnp.zeros_like(p_ext[:, pl.ds(at, 2), :, :])
            one = 0 if side == 0 else rows_x + 1
            vx[one] = jnp.zeros_like(vx[one])
            inv[one] = jnp.zeros_like(inv[one])

        @pl.when(jnp.logical_not(has[1, side]))
        def _(side=side):
            y_recv[:, side] = jnp.zeros_like(y_recv[:, side])
            yi_recv[side] = jnp.zeros_like(yi_recv[side])

        @pl.when(jnp.logical_not(has[2, side]))
        def _(side=side):
            z_recv[:, side] = jnp.zeros_like(z_recv[:, side])
            zi_recv[side] = jnp.zeros_like(zi_recv[side])

    lane = lax.broadcasted_iota(jnp.int32, (8, depth), 1)
    quad = lane & 3
    group = lane >> 2

    def packed(read):
        q = jnp.zeros((8, depth), F32)
        for j in range(rows_x * halves):
            rolled = pltpu.roll(read(j // halves, (j % halves) * 8), (4 * j + 2) % depth, 1)
            q = jnp.where(group == j, rolled, q)
        return q

    def coefs(level):
        first = root * depth
        last_ocean = level == first - 1
        crust = level == first
        up = jnp.where(crust, 1.0, 0.5).astype(F32)
        mid = jnp.where(last_ocean, 0.5, jnp.where(crust, -1.5, 0.0)).astype(F32)
        low = jnp.where(last_ocean, -1.0, jnp.where(crust, 0.5, -0.5)).astype(F32)
        return up, mid, low

    row_lane = lax.broadcasted_iota(jnp.int32, (1, 1, depth), 2)
    up, mid, low = coefs(me[2] * depth + row_lane)
    up_e, mid_e, low_e = coefs(
        jnp.where(quad == 1, me[2] * depth - 1, (me[2] + 1) * depth)
    )

    up_o, mid_o, low_o = coefs(
        me[2] * depth + jnp.where(quad < 2, depth - 2 + quad, quad - 2)
    )

    def copy_x(s, side, to):
        src, dst = (2, rows_x + 2) if side == 0 else (rows_x, 0)
        return pltpu.make_async_remote_copy(
            src_ref=p_ext.at[s, pl.ds(src, 2), y_in],
            dst_ref=p_ext.at[s, pl.ds(dst, 2), y_in],
            send_sem=send_sem.at[s, side],
            recv_sem=recv_sem.at[s, 1 - side],
            device_id=to,
            device_id_type=MESH_ID,
        )

    def copy_y(s, side, to):
        return pltpu.make_async_remote_copy(
            src_ref=y_send.at[s, side],
            dst_ref=y_recv.at[s, 1 - side],
            send_sem=send_sem.at[s, 2 + side],
            recv_sem=recv_sem.at[s, 3 - side],
            device_id=to,
            device_id_type=MESH_ID,
        )

    def copy_z(s, side, to):
        return pltpu.make_async_remote_copy(
            src_ref=z_send.at[s],
            dst_ref=z_recv.at[s, 1 - side],
            send_sem=send_sem.at[s, 4 + side],
            recv_sem=recv_sem.at[s, 5 - side],
            device_id=to,
            device_id_type=MESH_ID,
        )

    step_copies = {0: copy_x, 1: copy_y, 2: copy_z}

    def init_copy(src, dst, to, n, back):
        return pltpu.make_async_remote_copy(
            src_ref=src,
            dst_ref=dst,
            send_sem=init_send.at[n],
            recv_sem=init_recv.at[back],
            device_id=to,
            device_id_type=MESH_ID,
        )

    def init_copies(a, side, to):
        if a == 0:
            src, dst = (0, rows_x + 1) if side == 0 else (rows_x - 1, 0)
            return [
                init_copy(
                    v_in.at[0, pl.ds(src, 1)], vx.at[pl.ds(dst, 1)], to, side, 1 - side
                ),
                init_copy(
                    inv.at[pl.ds(src + 1, 1)], inv.at[pl.ds(dst, 1)], to, 6 + side, 7 - side
                ),
            ]
        if a == 1:
            return [init_copy(yi_send.at[side], yi_recv.at[1 - side], to, 2 + side, 3 - side)]
        return [init_copy(zi_send, zi_recv.at[1 - side], to, 4 + side, 5 - side)]

    def start_faces(s, axis):
        for f in faces:
            if f[0] == axis:

                @pl.when(has[f])
                def _(f=f):
                    step_copies[axis](s, f[1], other[f]).start()

    def send_x_y(s):
        start_faces(s, 0)
        y_send[s, 0] = p_ext[s, 2 : rows_x + 2, YA : YA + 2, :]
        y_send[s, 1] = p_ext[s, 2 : rows_x + 2, YA + rows_y - 2 : YA + rows_y, :]
        start_faces(s, 1)

    def send_z(s):
        z_send[s] = packed(lambda x, y: p_ext[s, 2 + x, pl.ds(YA + y, 8), :])
        start_faces(s, 2)

    def send(s):
        send_x_y(s)
        send_z(s)

    def receive(s):
        for f in faces:

            @pl.when(has[f])
            def _(f=f):
                step_copies[f[0]](s, 1 - f[1], other[f]).wait_recv()

    def pressure_rows(s, x, n, last):
        at = pl.ds(x, n)
        w = vz[at]
        above_v = pltpu.roll(jnp.where(row_lane == 0, 0.0, w), depth - 1, 2)
        below_v = pltpu.roll(jnp.where(row_lane == depth - 1, 0.0, w), 1, 2)
        spread = (
            0.5 * (vx[pl.ds(x + 2, n)] - vx[at])
            + 0.5 * (vy[at, pl.ds(YA + 1, rows_y), :] - vy[at, pl.ds(YA - 1, rows_y), :])
            + (up * above_v + mid * w + low * below_v)
        )
        added = jnp.where(row_lane == 0, pltpu.roll(source[at], (depth - s) % depth, 2), 0.0)
        new = p_ext[s, pl.ds(x + 2, n), y_in, :] - 0.5 * bulk[at] * spread + added
        if last:
            p_out[at] = new
        else:
            p_ext[s + 1, pl.ds(x + 2, n), y_in, :] = new

    def velocity_x(s, at, n):
        rows = pl.ds(at, n)
        vx[rows] = vx[rows] - 0.25 * inv[rows] * (
            p_ext[s, pl.ds(at + 2, n), y_in, :] - p_ext[s, rows, y_in, :]
        )

    near_edge = (lane < 2) | (lane >= depth - 2)

    def add_packed(value, ref, x_at, y_at):
        for j in range(rows_x * halves):
            rolled = pltpu.roll(value, (-(4 * j + 2)) % depth, 1)
            at = (x_at + j // halves, pl.ds(y_at + (j % halves) * 8, 8))
            ref[at] = ref[at] + jnp.where(near_edge, rolled, 0.0)

    chunk = 4

    def inner(s, last):
        half = (rows_x - 2) // 2
        velocity_x(s, 2, half)
        velocity_x(s, 2 + half, rows_x - 2 - half)
        for i in range(0, rows_x, chunk):
            at = pl.ds(i, chunk)
            at_p = pl.ds(i + 2, chunk)
            here = p_ext[s, at_p, y_in, :]
            rho = inv[pl.ds(i + 1, chunk)]
            vy[at, y_in, :] = vy[at, y_in, :] - 0.25 * rho * (
                p_ext[s, at_p, pl.ds(YA + 1, rows_y), :] - p_ext[s, at_p, pl.ds(YA - 1, rows_y), :]
            )
            above_p = pltpu.roll(jnp.where(row_lane == 0, 0.0, here), depth - 1, 2)
            below_p = pltpu.roll(jnp.where(row_lane == depth - 1, 0.0, here), 1, 2)
            vz[at] = vz[at] - 0.5 * rho * (up * above_p + mid * here + low * below_p)
        for i in range(2, rows_x - 2, chunk):
            pressure_rows(s, i, chunk, last)

    def outer(s, last):
        velocity_x(s, 0, 2)
        velocity_x(s, rows_x, 2)
        pressure_rows(s, 0, 2, last)
        pressure_rows(s, rows_x - 2, 2, last)

        ref, x_at, y_at = (p_out, 0, 0) if last else (p_ext.at[s + 1], 2, YA)
        rows = pl.ds(x_at, rows_x)
        for side, edge, after, sign in ((0, 0, 1, 0.25), (1, rows_y - 1, rows_y - 2, -0.25)):
            near = y_recv[s, side, :, 1 - side : 2 - side, :]
            far = y_recv[s, side, :, side : side + 1, :]
            halo_v = vy_edge[side] - sign * inv_y[side] * (
                y_send[s, side, :, side : side + 1, :] - far
            )
            vy_edge[side] = halo_v
            change = sign * inv[1 : rows_x + 1, edge : edge + 1, :] * near
            at_v = (slice(None), slice(YA + edge, YA + edge + 1), slice(None))
            vy[at_v] = vy[at_v] + change
            at_edge = (rows, pl.ds(y_at + edge, 1))
            ref[at_edge] = ref[at_edge] + sign * bulk[:, edge : edge + 1, :] * halo_v
            at_after = (rows, pl.ds(y_at + after, 1))
            ref[at_after] = ref[at_after] + sign * bulk[:, after : after + 1, :] * change

        own = z_send[s]
        halo = jnp.where(quad < 2, z_recv[s, 0], z_recv[s, 1])
        above = pltpu.roll(jnp.where(quad == 2, own, halo), depth - 1, 1)
        below = pltpu.roll(jnp.where(quad == 1, own, halo), 1, 1)
        edge = vz_edge[...] - 0.5 * pack_edge[...] * (
            up_e * above + mid_e * halo + low_e * below
        )
        vz_edge[...] = edge
        change = -0.5 * zi_send[1] * jnp.where(
            quad == 1,
            up_o * pltpu.roll(halo, depth - 1, 1),
            jnp.where(quad == 2, low_o * pltpu.roll(halo, 1, 1), 0.0),
        )
        vz_change[...] = change
        ahead = pltpu.roll(jnp.where(quad == 2, edge, change), depth - 1, 1)
        behind = pltpu.roll(jnp.where(quad == 1, edge, change), 1, 1)
        spread = jnp.where(quad < 2, up_o * ahead, low_o * behind) + mid_o * change
        add_packed(-0.5 * bulk_pack[...] * spread, ref, x_at, y_at)

    count = sum(has[f].astype(jnp.int32) for f in faces)
    count = count + jnp.where(at_sea, tiles - 1 + n_z - 1, 0)
    loads[0].wait()
    pl.semaphore_wait(barrier, count)
    send(0)
    for load in loads[1:]:
        load.wait()
    zi_send[0] = packed(lambda x, y: vz[x, pl.ds(y, 8), :])
    zi_send[1] = packed(lambda x, y: inv[1 + x, pl.ds(y, 8), :])
    for side, y in ((0, 0), (1, rows_y - 1)):
        yi_send[side, :, 0:1, :] = vy[:, YA + y : YA + y + 1, :]
        yi_send[side, :, 1:2, :] = inv[1 : rows_x + 1, y : y + 1, :]
    for f in faces:

        @pl.when(has[f])
        def _(f=f):
            for copy in init_copies(*f, other[f]):
                copy.start()

    cell_x = gx_ref[...] - me[0] * rows_x
    cell_y = gy_ref[...] - me[1] * rows_y
    inside = (cell_x >= 0) & (cell_x < rows_x) & (cell_y >= 0) & (cell_y < rows_y)
    cell = jnp.where(inside, cell_x * rows_y + cell_y, -1)
    gauges = cell.shape[1]

    def three_parts(value):
        high = value.astype(jnp.bfloat16).astype(F32)
        rest = value - high
        middle = rest.astype(jnp.bfloat16).astype(F32)
        return high, middle, rest - middle

    @pl.when(me[2] != 0)
    def _():
        source[...] = jnp.zeros_like(source)

    @pl.when(me[2] == 0)
    def _():
        hot = lax.broadcasted_iota(jnp.int32, (cells, gauges), 0) == cell
        hot = hot.astype(F32).astype(jnp.bfloat16)
        scaled = jnp.concatenate(
            [0.5 * misfit_ref[...], jnp.zeros((depth - ITERS, gauges), F32)], axis=0
        )
        planes = jnp.zeros((cells, depth), F32)
        for value in three_parts(scaled):
            planes = planes + lax.dot_general(
                hot, value.astype(jnp.bfloat16), NT, preferred_element_type=F32
            )
        source[...] = planes.reshape(rows_x, rows_y, depth)

    nodes = patch_ref.shape[-1]
    patches = slot_ref.shape[1]
    per = patches // tiles
    shift = per.bit_length() - 1
    assert per == 1 << shift and per == 128
    block = min(patches, 1024)

    def slot_tables():
        patch = patch_ref[...].reshape(1, nodes)
        slot_parts = jnp.zeros((8, nodes), F32)
        first_row = lax.broadcasted_iota(jnp.int32, (8, block), 0) == 0
        for at in range(0, patches, block):
            slots = slot_ref[:, at : at + block]
            table = jnp.where(first_row, slots >> shift, slots & (per - 1)).astype(F32)
            hot = lax.broadcasted_iota(jnp.int32, (block, nodes), 0) + at == patch
            slot_parts = slot_parts + jnp.dot(
                table.astype(jnp.bfloat16),
                hot.astype(F32).astype(jnp.bfloat16),
                preferred_element_type=F32,
            )
        slot = (slot_parts[0:1] * per + slot_parts[1:2]).astype(jnp.int32)
        for at in range(0, patches, block):
            hot = lax.broadcasted_iota(jnp.int32, (block, nodes), 0) + at == slot
            slot_hot[pl.ds(at, block), :] = hot.astype(F32).astype(jnp.bfloat16)
        node = lax.broadcasted_iota(jnp.int32, (depth, nodes), 1)
        spread_hot[...] = (
            lax.broadcasted_iota(jnp.int32, (depth, nodes), 0) == 4 * (node >> 3) + 2
        ).astype(F32).astype(jnp.bfloat16)

    def slip_copy(o_x, o_y, source_tile):
        return pltpu.make_async_remote_copy(
            src_ref=part.at[o_x * n_y + o_y],
            dst_ref=got.at[source_tile],
            send_sem=slip_send.at[o_x * n_y + o_y],
            recv_sem=slip_recv.at[source_tile],
            device_id=(o_x, o_y, me[2]),
            device_id_type=MESH_ID,
        )

    def depth_copy(c, slot):
        return pltpu.make_async_remote_copy(
            src_ref=total,
            dst_ref=got_all.at[slot],
            send_sem=depth_send.at[c],
            recv_sem=depth_recv.at[slot],
            device_id=(me[0], me[1], c),
            device_id_type=MESH_ID,
        )

    my_slot = jnp.where(me[2] >= root, 1, 0)

    def finish_sea(sea):
        @pl.when(at_sea)
        def _():
            mine = 0.5 * jnp.where(me[2] == root, sea, pltpu.roll(sea, 1, 1))
            values = jnp.dot(
                jnp.concatenate(three_parts(mine), axis=0).astype(jnp.bfloat16),
                spread_hot[...],
                preferred_element_type=F32,
            )
            values = values[0:8] + values[8:16] + values[16:24]
            sub = lax.broadcasted_iota(jnp.int32, (8, nodes), 0)
            col = lax.broadcasted_iota(jnp.int32, (8, nodes), 1)
            row = jnp.sum(jnp.where((col & 7) == sub, values, 0.0), axis=0, keepdims=True)
            row = row * weight_ref[...].reshape(1, nodes)
            high, middle, lowest = three_parts(row)
            split = jnp.where(
                sub == 0, high, jnp.where(sub == 1, middle, jnp.where(sub == 2, lowest, 0.0))
            ).astype(jnp.bfloat16)
            for at in range(0, patches, block):
                sums = lax.dot_general(
                    split, slot_hot[pl.ds(at, block), :], NT, preferred_element_type=F32
                )
                sums = jnp.sum(sums, axis=0, keepdims=True)
                for o in range(block // per):
                    part[at // per + o] = sums[:, o * per : (o + 1) * per]
            got[tile] = part[tile]
            each_tile(lambda o_x, o_y: slip_copy(o_x, o_y, tile).start())

    def owner_sums():
        @pl.when(at_sea)
        def _():
            each_tile(lambda o_x, o_y: slip_copy(o_x, o_y, o_x * n_y + o_y).wait_recv())
            total[...] = jnp.sum(got[...], axis=0)
            got_all[my_slot] = total[...]
            for c in range(n_z):

                @pl.when(me[2] != c)
                def _(c=c):
                    depth_copy(c, my_slot).start()

    bulk_pack[...] = packed(lambda x, y: bulk[x, pl.ds(y, 8), :])

    def receive_start():
        for f in faces:

            @pl.when(has[f])
            def _(f=f):
                for copy in init_copies(f[0], 1 - f[1], other[f]):
                    copy.wait_recv()

        for side in (0, 1):
            vy_edge[side] = yi_recv[side, :, 0:1, :]
            inv_y[side] = yi_recv[side, :, 1:2, :]
        kept = (quad == 1) | (quad == 2)
        vz_edge[...] = jnp.where(
            kept, jnp.where(quad == 1, zi_recv[0, 0], zi_recv[1, 0]), 0.0
        )
        pack_edge[...] = jnp.where(
            kept, jnp.where(quad == 1, zi_recv[0, 1], zi_recv[1, 1]), 0.0
        )

    sea = z_send[0]
    for s in range(ITERS):
        last = s == ITERS - 1
        if s > 0:
            if last:
                send_z(s)
                finish_sea(sea + z_send[s])
                send_x_y(s)
            else:
                send(s)
                sea = sea + z_send[s]
            add_packed(vz_change[...], vz, 0, 0)
        inner(s, last)
        if s == 1:
            pl.when(at_sea)(slot_tables)
        receive(s)
        if s == 0:
            receive_start()
        if last:
            owner_sums()
        outer(s, last)
    add_packed(vz_change[...], vz, 0, 0)
    v_out[0] = vx[1 : rows_x + 1]
    v_out[1] = vy[:, YA : YA + rows_y, :]
    v_out[2] = vz[...]

    for slot_at, c in ((0, root - 1), (1, root)):

        @pl.when(me[2] != c)
        def _(slot_at=slot_at):
            depth_copy(0, slot_at).wait_recv()

    sums = got_all[0] + got_all[1]
    piece = per // n_z
    picked = sums[:, 0:piece]
    for c in range(1, n_z):
        picked = jnp.where(me[2] == c, sums[:, c * piece : (c + 1) * piece], picked)
    slip_out[...] = picked

    for f in faces:

        @pl.when(has[f])
        def _(f=f):
            for copy in init_copies(*f, other[f]):
                copy.wait_send()
            for s in range(ITERS):
                step_copies[f[0]](s, f[1], other[f]).wait_send()

    @pl.when(at_sea)
    def _():
        each_tile(lambda o_x, o_y: slip_copy(o_x, o_y, tile).wait_send())
        for c in range(n_z):

            @pl.when(me[2] != c)
            def _(c=c):
                depth_copy(c, my_slot).wait_send()


def write_out(p_in, v_in, slip_in, p_out, v_out, slip_out, sem):
    copies = [
        pltpu.make_async_copy(src, dst, sem.at[n])
        for n, (src, dst) in enumerate([(v_in, v_out), (p_in, p_out), (slip_in, slip_out)])
    ]
    for copy in copies:
        copy.start()
    for copy in copies:
        copy.wait()


def local(sizes, pressure, velocity, inv_density, bulk, node_weight, node_patch, patch_slot,
          gauge_x, gauge_y, gauge_misfit):
    rows_x, rows_y, depth = pressure.shape
    n_x, n_y, n_z = sizes
    tiles = n_x * n_y
    nodes = node_patch.shape[-1]
    patches = patch_slot.shape[0]
    per = patches // tiles
    wide_y = rows_y + 2 * YA
    box = (rows_x, rows_y, depth)
    vmem = pl.BlockSpec(memory_space=pltpu.VMEM)
    hbm = pl.BlockSpec(memory_space=pltpu.HBM)
    gauges = gauge_x.shape[0]
    scratch = [
        pltpu.VMEM((1, 1, nodes), F32),
        pltpu.VMEM((1, 1, nodes), jnp.int32),
        pltpu.VMEM((1, patches), jnp.int32),
        pltpu.VMEM((1, gauges), jnp.int32),
        pltpu.VMEM((1, gauges), jnp.int32),
        pltpu.VMEM((ITERS, gauges), F32),
        pltpu.VMEM((ITERS, rows_x + 4, wide_y, depth), F32),
        pltpu.VMEM((rows_x + 2, rows_y, depth), F32),
        pltpu.VMEM((rows_x, wide_y, depth), F32),
        pltpu.VMEM(box, F32),
        pltpu.VMEM((rows_x + 2, rows_y, depth), F32),
        pltpu.VMEM((2, rows_x, 1, depth), F32),
        pltpu.VMEM(box, F32),
        pltpu.VMEM((8, depth), F32),
        pltpu.VMEM((8, depth), F32),
        pltpu.VMEM((2, rows_x, 1, depth), F32),
        pltpu.VMEM((8, depth), F32),
        pltpu.VMEM((8, depth), F32),
        pltpu.VMEM((ITERS, 2, rows_x, 2, depth), F32),
        pltpu.VMEM((ITERS, 2, rows_x, 2, depth), F32),
        pltpu.VMEM((ITERS, 8, depth), F32),
        pltpu.VMEM((ITERS, 2, 8, depth), F32),
        pltpu.VMEM((2, rows_x, 2, depth), F32),
        pltpu.VMEM((2, rows_x, 2, depth), F32),
        pltpu.VMEM((2, 8, depth), F32),
        pltpu.VMEM((2, 2, 8, depth), F32),
        pltpu.VMEM(box, F32),
        pltpu.VMEM((patches, nodes), jnp.bfloat16),
        pltpu.VMEM((depth, nodes), jnp.bfloat16),
        pltpu.VMEM((tiles, 1, per), F32),
        pltpu.VMEM((tiles, 1, per), F32),
        pltpu.VMEM((1, per), F32),
        pltpu.VMEM((2, 1, per), F32),
        pltpu.SemaphoreType.DMA((12,)),
        pltpu.SemaphoreType.DMA((ITERS, 6)),
        pltpu.SemaphoreType.DMA((ITERS, 6)),
        pltpu.SemaphoreType.DMA((8,)),
        pltpu.SemaphoreType.DMA((8,)),
        pltpu.SemaphoreType.DMA((tiles,)),
        pltpu.SemaphoreType.DMA((tiles,)),
        pltpu.SemaphoreType.DMA((n_z,)),
        pltpu.SemaphoreType.DMA((2,)),
    ]
    colored = [pltpu.VMEM(box, F32), pltpu.VMEM((3,) + box, F32), pltpu.VMEM((1, per // n_z), F32)]
    shapes = [
        jax.ShapeDtypeStruct(box, F32),
        jax.ShapeDtypeStruct((3,) + box, F32),
        jax.ShapeDtypeStruct((1, per // n_z), F32),
    ]
    p_new, v_new, slip = pl.pallas_call(
        functools.partial(kernel, sizes),
        out_shape=colored,
        in_specs=[hbm] * 10,
        out_specs=[vmem] * 3,
        scratch_shapes=scratch,
        compiler_params=pltpu.CompilerParams(
            collective_id=0, has_side_effects=True, vmem_limit_bytes=64 * 1024 * 1024 - 1400 * 1024
        ),
    )(
        pressure,
        velocity,
        inv_density,
        bulk,
        node_weight,
        node_patch,
        patch_slot.reshape(1, patches),
        gauge_x.reshape(1, -1),
        gauge_y.reshape(1, -1),
        gauge_misfit,
    )
    anywhere = pl.BlockSpec(memory_space=pl.ANY)
    p_new, v_new, slip = pl.pallas_call(
        write_out,
        out_shape=shapes,
        in_specs=[anywhere] * 3,
        out_specs=[anywhere] * 3,
        scratch_shapes=[pltpu.SemaphoreType.DMA((3,))],
        compiler_params=pltpu.CompilerParams(vmem_limit_bytes=2 * 1024 * 1024),
    )(p_new, v_new, slip)
    return p_new, v_new, slip.reshape(per // n_z)


def solution(mesh):
    placed = (
        P("gx", "gy", "gz"),
        P(None, "gx", "gy", "gz"),
        P("gx", "gy", "gz"),
        P("gx", "gy", "gz"),
        P("gx", "gy", None),
        P("gx", "gy", None),
        P(),
        P(),
        P(),
        P(),
    )
    sizes = tuple(mesh.shape[a] for a in AXES)
    return jax.shard_map(
        functools.partial(local, sizes),
        mesh=mesh,
        in_specs=placed,
        out_specs=(P("gx", "gy", "gz"), P(None, "gx", "gy", "gz"), P(("gx", "gy", "gz"))),
        check_vma=False,
    )
```
